32 devices in a mesh: gz: 8 (over y, x, core), xy: 4 (over z).
Axes of the slice: x: 2, y: 2, z: 4, core: 2. Of those that a mesh axis runs over, the one named last changes fastest.
Arguments:
- raw_volume: bfloat16 [16, 512, 512], P('gz', 'xy'), may hold values from -6 to 6
- weight_first: bfloat16 [32, 1, 3, 3], replicated, may hold values from -3 to 3
- bias_first: float32 [32], replicated, may hold values from -3 to 3
- weight_second: bfloat16 [64, 32, 3, 3], replicated, may hold values from -0.5 to 0.5
- bias_second: float32 [64], replicated, may hold values from -3 to 3
- weight_third: bfloat16 [128, 64, 3, 3], replicated, may hold values from -0.375 to 0.375
- bias_third: float32 [128], replicated, may hold values from -3 to 3
- weight_iso_a: bfloat16 [3, 3, 3, 128, 256], replicated, may hold values from -0.15625 to 0.15625
- bias_iso_a: float32 [256], replicated, may hold values from -3 to 3
- weight_iso_b: bfloat16 [3, 3, 3, 256, 256], replicated, may hold values from -0.109375 to 0.109375
- bias_iso_b: float32 [256], replicated, may hold values from -3 to 3
Outputs:
- features: bfloat16 [16, 64, 64, 256], P(None, 'xy', 'gz')
The draws below stay inside these ranges and needn't reach their ends.
All inputs are finite; a program needn't handle non-finite values.
Results may differ from the reference program's by a relative error of at most 0.0069.
Values may be sent and summed in bfloat16 or wider, within the bound.
No kernel may reach another device: no remote copies, remote signals or barrier semaphores. Data moves between devices by JAX's collectives and lax.ppermute only.
A program may use at most 128 MiB of HBM per device.

```python
import jax
import jax.numpy as jnp
from jax import lax

H = 512
W = 512
C0 = 32
C1 = 64
C2 = 128
C3 = 256
Z = 16


def block_scale(stream_key, shape, shards, least, high):
    loudness = 1.0
    for position, blocks in shards:
        draws = jax.random.uniform(jax.random.fold_in(jax.random.fold_in(stream_key, 6), position), (blocks,), jnp.float32, least / len(shards), high / len(shards))
        loudness = loudness * jnp.repeat(jnp.exp(draws), shape[position] // blocks).reshape((-1,) + (1,) * (len(shape) - 1 - position))
    return loudness


def bell_draw(stream_key, dims, deviation, most, shards=(), held_as=jnp.bfloat16):
    values = deviation * jax.random.normal(stream_key, dims, jnp.float32)
    if shards:
        values = values * block_scale(stream_key, dims, shards, -0.22, 0.18)
    return jnp.clip(values, -most, most).astype(held_as)


def setup_inputs(seed: int = 0) -> dict:
    seeds = jax.random.split(jax.random.key(seed), 12)
    raw_volume = bell_draw(seeds[0], (Z, H, W), 1.0, 6.0, ((0, 8), (1, 4)))
    weight_first = bell_draw(seeds[1], (C0, 1, 3, 3), 4 ** -0.5, 3.0)
    bias_first = bell_draw(seeds[2], (C0,), 0.3, 3.0, (), jnp.float32)
    weight_second = bell_draw(seeds[3], (C1, C0, 3, 3), (9 * C0 // 2) ** -0.5, 0.5)
    bias_second = bell_draw(seeds[4], (C1,), 0.3, 3.0, (), jnp.float32)
    weight_third = bell_draw(seeds[5], (C2, C1, 3, 3), (9 * C1 // 2) ** -0.5, 0.375)
    bias_third = bell_draw(seeds[6], (C2,), 0.3, 3.0, (), jnp.float32)
    weight_iso_a = bell_draw(seeds[7], (3, 3, 3, C2, C3), (27 * C2 // 2) ** -0.5, 0.15625)
    bias_iso_a = bell_draw(seeds[8], (C3,), 0.3, 3.0, (), jnp.float32)
    weight_iso_b = bell_draw(seeds[9], (3, 3, 3, C3, C3), (27 * C3 // 2) ** -0.5, 0.109375)
    bias_iso_b = bell_draw(seeds[10], (C3,), 0.3, 3.0, (), jnp.float32)
    return {"raw_volume": raw_volume, "weight_first": weight_first, "bias_first": bias_first, "weight_second": weight_second, "bias_second": bias_second, "weight_third": weight_third, "bias_third": bias_third, "weight_iso_a": weight_iso_a, "bias_iso_a": bias_iso_a, "weight_iso_b": weight_iso_b, "bias_iso_b": bias_iso_b}


def pool_plane(values):
    sections, chans, height, breadth = values.shape
    return values.reshape(sections, chans, height // 2, 2, breadth // 2, 2).max(axis=(3, 5))


def plane_level(stack, weight, bias):
    def one_section(section):
        out = lax.conv_general_dilated(section[None].astype(jnp.float32), weight.astype(jnp.float32), (1, 1), ((1, 1), (1, 1)), dimension_numbers=("NCHW", "OIHW", "NCHW"), precision=lax.Precision.HIGHEST)
        out = out[0] + bias[:, None, None]
        return jnp.maximum(out, 0.0).astype(jnp.bfloat16)
    return pool_plane(lax.map(one_section, stack))


def cube_level(volume, weight, bias):
    out = lax.conv_general_dilated(volume[None].astype(jnp.float32), weight.astype(jnp.float32), (1, 1, 1), ((1, 1), (1, 1), (1, 1)), dimension_numbers=("NDHWC", "DHWIO", "NDHWC"), precision=lax.Precision.HIGHEST)
    return jnp.maximum(out[0] + bias, 0.0).astype(jnp.bfloat16)


def reference(raw_volume, weight_first, bias_first, weight_second, bias_second, weight_third, bias_third, weight_iso_a, bias_iso_a, weight_iso_b, bias_iso_b):
    stack = raw_volume[:, None, :, :]
    stack = plane_level(stack, weight_first, bias_first)
    stack = plane_level(stack, weight_second, bias_second)
    stack = plane_level(stack, weight_third, bias_third)
    volume = jnp.transpose(stack, (0, 2, 3, 1))
    middle = cube_level(volume, weight_iso_a, bias_iso_a)
    return cube_level(middle, weight_iso_b, bias_iso_b)
```

```python
import functools

import jax
import jax.numpy as jnp
from jax import lax
from jax.experimental import pallas as pl
from jax.experimental.pallas import tpu as pltpu
from jax.sharding import PartitionSpec as P

HALO = 24
VMEM = pl.BlockSpec(memory_space=pltpu.VMEM)
F32 = jnp.float32
BF16 = jnp.bfloat16


def lane_iota(shape):
    return lax.broadcasted_iota(jnp.int32, shape, len(shape) - 1)


def shift_rows(x, down):
    sub = lax.broadcasted_iota(jnp.int32, x.shape, 2)
    if down:
        rolled = pltpu.roll(x, 1, 2)
        other = jnp.concatenate([rolled[:, -1:], rolled[:, :-1]], axis=1)
        return jnp.where(sub == 0, other, rolled)
    rolled = pltpu.roll(x, 7, 2)
    other = jnp.concatenate([rolled[:, 1:], rolled[:, :1]], axis=1)
    return jnp.where(sub == 7, other, rolled)


def tile_lanes(ref, row):
    x = ref[row : row + 1, :]
    return x + pltpu.roll(x, 32, 1) + pltpu.roll(x, 64, 1) + pltpu.roll(x, 96, 1)


def plane_kernel(
    cfg, lo, raw, hi, w1, b1, w2, b2, w3, b3, out,
    rs, small, t1, t2, t3, dd, ff, ppe, ppo,
):
    zl, rows, width, dests, vb = cfg
    third_rows = rows // 8
    tiles = third_rows // 8 + 1
    period = tiles * 8
    m = zl * period
    groups = width // 16 + 1
    first = lax.axis_index("xy") == 0
    last = lax.axis_index("xy") == lax.axis_size("xy") - 1
    sub8 = lax.broadcasted_iota(jnp.int32, (1, 1, 8, 128), 2)
    keep = jnp.where(sub8 < 4, jnp.where(last, 0.0, 1.0), jnp.where(first, 0.0, 1.0))

    def masked(x):
        n, lanes = x.shape
        x = x.reshape(n // period, tiles, 8, lanes)
        k = jnp.concatenate([keep] * (lanes // 128), axis=3)
        return jnp.concatenate([x[:, :-1], x[:, -1:] * k], axis=1)

    for z in range(zl):
        lo32 = lo[z].astype(F32)
        raw32 = raw[z].astype(F32)
        end = 8 + 8 * period
        rs[z, 0] = jnp.zeros((end + 8, 128), F32)
        rs[z, width // 128 + 1] = jnp.zeros((end + 8, 128), F32)
        hi32 = hi[z].astype(F32)
        for t in range(width // 128):
            cols = slice(128 * t, 128 * t + 128)
            rs[z, t + 1, 0:8] = lo32[HALO - 8 :, cols]
            rs[z, t + 1, 8 : 8 + rows] = raw32[:, cols]
            rs[z, t + 1, 8 + rows : 8 + rows + HALO] = hi32[:, cols]
            rs[z, t + 1, 8 + rows + HALO : end - HALO] = jnp.zeros((8 * period - rows - 2 * HALO, 128), F32)
            rs[z, t + 1, end - HALO : end] = lo32[:, cols]
            rs[z, t + 1, end : end + 8] = raw32[0:8, cols]

    small[...] = jnp.zeros_like(small)
    for ky in range(3):
        small[3 * ky : 3 * ky + 3, 0:32] = w1[ky].astype(F32)
    small[9:10, 0:32] = b1[...]
    small[10:11, 0:64] = b2[...]
    tap = []
    for i in range(10):
        x = tile_lanes(small, i)
        tap.append(jnp.concatenate([x, x], axis=1))
    bias1 = tap[9]
    x = small[10:11, :]
    bias2 = x + pltpu.roll(x, 64, 1)
    bias3 = b3[...]
    t1[...] = jnp.zeros_like(t1)
    gap = lax.broadcasted_iota(jnp.int32, (32, 256), 0) - 2 * (lane_iota((32, 256)) // 32)
    for ky in range(3):
        for dx in range(2):
            band = jnp.zeros((32, 256), F32)
            for kx in range(3):
                band = jnp.where(gap == dx + kx, tap[3 * ky + kx], band)
            band = band.astype(BF16)
            for dy in range(2):
                phase = 2 * dy + dx
                t1[64 * (ky + dy) : 64 * (ky + dy) + 32, 256 * phase : 256 * phase + 256] = band

    t2[...] = jnp.zeros_like(t2)
    t3[...] = jnp.zeros_like(t3)
    for ky in range(3):
        for kx in range(3):
            w = w2[ky, kx]
            for dy in range(2):
                for dx in range(2):
                    r, c = ky + dy, kx + dx
                    lanes = slice(128 * dy + 64 * dx, 128 * dy + 64 * dx + 64)
                    t2[0, 128 * r + 32 * c : 128 * r + 32 * c + 32, lanes] = w
                    c = (c + 2) % 4
                    t2[1, 128 * r + 32 * c : 128 * r + 32 * c + 32, lanes] = w
            w = w3[ky, kx]
            for dx in range(2):
                at = 256 * ky + 64 * (kx + dx)
                t3[at : at + 64, 128 * dx : 128 * dx + 128] = w

    lane = lane_iota((period, 128))
    for g in range(groups):
        start = 16 * g + 125
        t, s = start // 128, start % 128
        left = 128 - s
        for z in range(zl):
            for k in range(5):
                def piece(phase, tile, amount):
                    x = rs[z, tile, pl.ds(8 + phase, period, stride=8), :]
                    return pltpu.roll(x, amount % 128, 1)

                a = piece(2 * k - 1, t, -s)
                b = piece(2 * k, t, 64 - s)
                if left < 18:
                    a = jnp.where(lane < left, a, piece(2 * k - 1, t + 1, -s))
                    b = jnp.where(lane < 64 + left, b, piece(2 * k, t + 1, 64 - s))
                dd[k, g * m + z * period : g * m + z * period + period, :] = jnp.where(lane < 64, a, b).astype(BF16)

    chunk = 11 if groups % 11 == 0 else 1
    n = chunk * m
    for m1 in range(4):
        def level1(c, _, m1=m1):
            at = pl.multiple_of(c * n, 16)
            x = jnp.concatenate([dd[m1, pl.ds(at, n), :], dd[m1 + 1, pl.ds(at, n), :]], axis=1)
            acc = None
            for phase in range(4):
                y = jnp.dot(x, t1[:, 256 * phase : 256 * phase + 256], preferred_element_type=F32)
                acc = y if acc is None else jnp.maximum(acc, y)
            y = masked(jnp.maximum(acc + bias1, 0.0))
            row = pl.multiple_of(m + c * n, 16)
            ff[m1 + 1, pl.ds(row, n), :] = y.reshape(n, 256).astype(BF16)
            if m1 == 0:
                ff[5, pl.ds(row, n), :] = shift_rows(y, False).reshape(n, 256).astype(BF16)
            if m1 == 3:
                ff[0, pl.ds(row, n), :] = shift_rows(y, True).reshape(n, 256).astype(BF16)
            return 0

        lax.fori_loop(0, groups // chunk, level1, 0)
    for f in range(6):
        ff[f, 0:m, :] = jnp.zeros((m, 256), BF16)
        x = ff[f, m : 2 * m, 0:128].astype(F32)
        ff[f, m : 2 * m, 0:128] = jnp.where(lane_iota((m, 128)) < 32, 0.0, x).astype(BF16)
        x = ff[f, groups * m : (groups + 1) * m, 0:128].astype(F32)
        ff[f, groups * m : (groups + 1) * m, 0:128] = jnp.where(lane_iota((m, 128)) < 32, x, 0.0).astype(BF16)
        ff[f, groups * m : (groups + 1) * m, 128:256] = jnp.zeros((m, 128), BF16)

    def half(f, at, n, lanes):
        return ff[f, pl.ds(pl.multiple_of(at, 16), n), lanes : lanes + 128]

    def swapped(f, at_low, low, at_high, high, n):
        mask = lane_iota((n, 128)) < 64
        return jnp.where(mask, half(f, at_low, n, low), half(f, at_high, n, high))

    def level2(m2, at, n, even):
        low, high = [], []
        for r in range(4):
            f = 2 * m2 + r
            if even:
                low.append(swapped(f, at, 0, at - m, 128, n))
                high.append(half(f, at, n, 0))
            else:
                low.append(swapped(f, at, 128, at, 0, n))
                high.append(half(f, at, n, 128))
        low = jnp.dot(jnp.concatenate(low, axis=1), t2[1], preferred_element_type=F32)
        high = jnp.dot(jnp.concatenate(high, axis=1), t2[0], preferred_element_type=F32)
        low = jnp.maximum(low[:, :128], low[:, 128:])
        high = jnp.maximum(high[:, :128], high[:, 128:])
        mask = lane_iota((n, 128)) < 64
        y = jnp.maximum(jnp.where(mask, low, high), pltpu.roll(jnp.where(mask, high, low), 64, 1))
        return masked(jnp.maximum(y + bias2, 0.0))

    for even, pp, count in ((True, ppe, groups), (False, ppo, groups - 1)):
        chunk = 11 if count % 11 == 0 else 8 if count % 8 == 0 else 1
        n = chunk * m
        for m2 in range(2):
            def step(c, _, m2=m2, even=even, pp=pp, n=n):
                at = pl.multiple_of(c * n, 16)
                y = level2(m2, at + m, n, even)
                pp[m2 + 1, pl.ds(at, n), :] = y.reshape(n, 128).astype(BF16)
                if m2 == 0:
                    pp[3, pl.ds(at, n), :] = shift_rows(y, False).reshape(n, 128).astype(BF16)
                else:
                    pp[0, pl.ds(at, n), :] = shift_rows(y, True).reshape(n, 128).astype(BF16)
                return 0

            lax.fori_loop(0, count // chunk, step, 0)
    for s in range(4):
        x = ppe[s, 0:m, :].astype(F32)
        ppe[s, 0:m, :] = jnp.where(lane_iota((m, 128)) < 64, 0.0, x).astype(BF16)
        at = (groups - 1) * m
        x = ppe[s, at : at + m, :].astype(F32)
        ppe[s, at : at + m, :] = jnp.where(lane_iota((m, 128)) < 64, x, 0.0).astype(BF16)

    def level3(at, n, odd):
        acc = None
        for dy in range(2):
            x = []
            for r in range(3):
                here = pl.ds(pl.multiple_of(at, 16), n)
                after = pl.ds(pl.multiple_of(at + m, 16), n)
                x += [ppo[dy + r, here, :], ppe[dy + r, after, :]] if odd else [ppe[dy + r, here, :], ppo[dy + r, here, :]]
            y = jnp.dot(jnp.concatenate(x, axis=1), t3[...], preferred_element_type=F32)
            y = jnp.maximum(y[:, :128], y[:, 128:])
            acc = y if acc is None else jnp.maximum(acc, y)
        y = masked(jnp.maximum(acc + bias3, 0.0))
        return y.reshape(n // m, zl, tiles, 8, 128)

    zero = jnp.zeros((2 * (tiles - 1) + 1, zl * 8, 128), BF16)
    out[0, 0] = zero
    out[dests - 1, vb + 1] = zero
    chunk = 8
    n = chunk * m
    for c in range((groups - 1) // chunk):
        ys = [level3(c * n, n, odd) for odd in (False, True)]
        a, b = [y[:, :, tiles - 1].reshape(chunk * zl, 8, 128) for y in ys]
        sub = lax.broadcasted_iota(jnp.int32, a.shape, 1)
        edge = jnp.where(sub < 4, pltpu.roll(a, 2, 1), pltpu.roll(b, 6, 1))
        edge = edge.reshape(chunk, zl * 8, 128).astype(BF16)
        mains = [y[:, :, i].reshape(chunk, zl * 8, 128).astype(BF16) for y in ys for i in range(tiles - 1)]
        for w in range(chunk):
            v = c * chunk + w
            for d in range(dests):
                at = v - (vb * d - 1)
                if 0 <= at < vb + 2:
                    for i, part in enumerate(mains + [edge]):
                        out[d, at, i] = part[w]


def cube_kernel(cfg, recv, wa, ba, wb, bb, out, wav, wbv, a3, b3, sems):
    sources, zl, third_rows, vb, in_chan, mid_chan, out_chan, flip = cfg
    depth = sources * zl
    xs = 2 * vb
    tiles = third_rows // 8
    copy_a = pltpu.make_async_copy(wa, wav, sems.at[0])
    copy_b = pltpu.make_async_copy(wb, wbv, sems.at[1])
    copy_a.start()
    copy_b.start()

    rows = 8 * depth
    shape = (rows, rows)
    to = lax.broadcasted_iota(jnp.int32, shape, 0)
    at = lax.broadcasted_iota(jnp.int32, shape, 1)
    k_to, z_to = to // depth, to % depth
    k_at, z_at = at % 8, (at // (8 * zl)) * zl + (at // 8) % zl
    gather = jnp.concatenate(
        [jnp.where((k_to == k_at) & (z_at == z_to + dz), 1.0, 0.0).astype(BF16) for dz in (-1, 0, 1)], axis=0
    )
    parts = 2 * tiles + 1
    for vl in range(vb + 2):
        for c in range(parts):
            x = recv[:, vl, c].reshape(rows, in_chan)
            y = jnp.dot(gather, x, preferred_element_type=F32).astype(BF16).reshape(3, 8, depth, in_chan)
            for dz in range(3):
                lanes = slice(dz * in_chan, (dz + 1) * in_chan)
                if c < 2 * tiles:
                    x_at, y_at = 2 * vl + c // tiles, 2 + 8 * (c % tiles)
                    a3[y_at : y_at + 8, x_at, :, lanes] = y[dz]
                else:
                    for side in range(2):
                        a3[0:2, 2 * vl + side, :, lanes] = y[dz, 4 * side : 4 * side + 2]
                        a3[third_rows + 2 : third_rows + 4, 2 * vl + side, :, lanes] = y[dz, 4 * side + 2 : 4 * side + 4]

    copy_a.wait()
    taps = [(ky, kx) for ky in range(3) for kx in range(3)]
    mid_x = xs + 2
    mid_rows = third_rows + 2
    step_rows = 9 if mid_rows % 9 == 0 else 1

    def iso_a(c, _):
        y0 = c * step_rows
        n = step_rows * mid_x * depth
        x = jnp.concatenate(
            [a3[pl.ds(y0 + ky, step_rows), kx : kx + mid_x].reshape(n, 3 * in_chan) for ky, kx in taps], axis=1
        )
        w = jnp.concatenate([wav[dz, ky, kx] for ky, kx in taps for dz in range(3)], axis=0)
        y = jnp.dot(x, w, preferred_element_type=F32)
        y = jnp.maximum(y + ba[...], 0.0)
        here = (step_rows, mid_x, depth, mid_chan)
        b3[pl.ds(y0, step_rows), :, :, mid_chan : 2 * mid_chan] = y.reshape(here).astype(BF16)
        y = y.reshape(step_rows * mid_x, depth // 8, 8, mid_chan)
        sub = lax.broadcasted_iota(jnp.int32, y.shape, 2)
        none = jnp.zeros_like(y[:, :1])
        rolled = pltpu.roll(y, 1, 2)
        other = jnp.concatenate([none, rolled[:, :-1]], axis=1)
        down = jnp.where(sub == 0, other, rolled)
        b3[pl.ds(y0, step_rows), :, :, 0:mid_chan] = down.reshape(here).astype(BF16)
        rolled = pltpu.roll(y, 7, 2)
        other = jnp.concatenate([rolled[:, 1:], none], axis=1)
        up = jnp.where(sub == 7, other, rolled)
        b3[pl.ds(y0, step_rows), :, :, 2 * mid_chan : 3 * mid_chan] = up.reshape(here).astype(BF16)
        return 0

    lax.fori_loop(0, mid_rows // step_rows, iso_a, 0)

    row, col = lax.axis_index("xy"), lax.axis_index("gz")

    @pl.when(row == 0)
    def _():
        b3[0] = jnp.zeros(b3.shape[1:], BF16)

    @pl.when(row == lax.axis_size("xy") - 1)
    def _():
        b3[mid_rows - 1] = jnp.zeros(b3.shape[1:], BF16)

    @pl.when(col == 0)
    def _():
        b3[:, 0] = jnp.zeros((mid_rows,) + b3.shape[2:], BF16)

    @pl.when(col == lax.axis_size("gz") - 1)
    def _():
        b3[:, mid_x - 1] = jnp.zeros((mid_rows,) + b3.shape[2:], BF16)

    copy_b.wait()
    if flip:
        n = xs * depth
        to = lax.broadcasted_iota(jnp.int32, (n, n), 0)
        at = lax.broadcasted_iota(jnp.int32, (n, n), 1)
        turn = jnp.where((to // xs == at % depth) & (to % xs == at // depth), 1.0, 0.0).astype(BF16)
    out_rows = 8

    def iso_b(c, _):
        y0 = c * out_rows
        n = out_rows * xs * depth
        x = jnp.concatenate(
            [b3[pl.ds(y0 + ky, out_rows), kx : kx + xs].reshape(n, 3 * mid_chan) for ky, kx in taps], axis=1
        )
        w = jnp.concatenate([wbv[dz, ky, kx] for ky, kx in taps for dz in range(3)], axis=0)
        y = jnp.dot(x, w, preferred_element_type=F32)
        y = jnp.maximum(y + bb[...], 0.0).astype(BF16)
        if flip:
            y = y.reshape(out_rows, xs * depth, out_chan)
            for i in range(out_rows):
                t = jnp.dot(turn, y[i], preferred_element_type=F32).astype(BF16)
                out[:, y0 + i] = t.reshape(depth, xs, out_chan)
        else:
            out[pl.ds(y0, out_rows)] = y.reshape(out_rows, xs, depth, out_chan)
        return 0

    lax.fori_loop(0, third_rows // out_rows, iso_b, 0)


def body(
    raw_volume,
    weight_first,
    bias_first,
    weight_second,
    bias_second,
    weight_third,
    bias_third,
    weight_iso_a,
    bias_iso_a,
    weight_iso_b,
    bias_iso_b,
):
    zl, rows, width = raw_volume.shape
    dests = lax.axis_size("gz")
    depth = zl * dests
    third_rows = rows // 8
    vb = width // 8 // dests // 2
    count = lax.axis_size("xy")
    forward = [(i, i + 1) for i in range(count - 1)]
    backward = [(i + 1, i) for i in range(count - 1)]
    lo = lax.ppermute(raw_volume[:, rows - HALO :], "xy", forward)
    hi = lax.ppermute(raw_volume[:, :HALO], "xy", backward)

    period = third_rows + 8
    m = zl * period
    groups = width // 16 + 1
    parts = 2 * (third_rows // 8) + 1
    send = pl.pallas_call(
        functools.partial(plane_kernel, (zl, rows, width, dests, vb)),
        out_shape=jax.ShapeDtypeStruct((dests, vb + 2, parts, zl * 8, 128), BF16),
        in_specs=[VMEM] * 9,
        out_specs=VMEM,
        scratch_shapes=[
            pltpu.VMEM((zl, width // 128 + 2, 8 * period + 16, 128), F32),
            pltpu.VMEM((16, 128), F32),
            pltpu.VMEM((256, 1024), BF16),
            pltpu.VMEM((2, 512, 256), BF16),
            pltpu.VMEM((768, 256), BF16),
            pltpu.VMEM((5, groups * m, 128), BF16),
            pltpu.VMEM((6, (groups + 1) * m, 256), BF16),
            pltpu.VMEM((4, groups * m, 128), BF16),
            pltpu.VMEM((4, (groups - 1) * m, 128), BF16),
        ],
        compiler_params=pltpu.CompilerParams(vmem_limit_bytes=60 << 20),
        name="planes",
    )(
        lo, raw_volume, hi,
        jnp.transpose(weight_first, (1, 2, 3, 0))[0], bias_first[None],
        jnp.transpose(weight_second, (2, 3, 1, 0)), bias_second[None],
        jnp.transpose(weight_third, (2, 3, 1, 0)), bias_third[None],
    )
    recv = lax.all_to_all(send, "gz", split_axis=0, concat_axis=0, tiled=True)

    xs = 2 * vb
    in_chan, mid_chan = weight_iso_a.shape[3:]
    out_chan = weight_iso_b.shape[4]
    flip = xs % 8 == 0
    shape = (depth, third_rows, xs, out_chan) if flip else (third_rows, xs, depth, out_chan)
    anywhere = pl.BlockSpec(memory_space=pl.ANY)
    out = pl.pallas_call(
        functools.partial(cube_kernel, (dests, zl, third_rows, vb, in_chan, mid_chan, out_chan, flip)),
        out_shape=jax.ShapeDtypeStruct(shape, BF16),
        in_specs=[VMEM, anywhere, VMEM, anywhere, VMEM],
        out_specs=VMEM,
        scratch_shapes=[
            pltpu.VMEM(weight_iso_a.shape, BF16),
            pltpu.VMEM(weight_iso_b.shape, BF16),
            pltpu.VMEM((third_rows + 4, xs + 4, depth, 3 * in_chan), BF16),
            pltpu.VMEM((third_rows + 2, xs + 2, depth, 3 * mid_chan), BF16),
            pltpu.SemaphoreType.DMA((2,)),
        ],
        compiler_params=pltpu.CompilerParams(vmem_limit_bytes=60 << 20),
        name="cubes",
    )(recv, weight_iso_a, bias_iso_a[None], weight_iso_b, bias_iso_b[None])
    return out if flip else jnp.transpose(out, (2, 0, 1, 3))


def solution(mesh):
    placed = (P("gz", "xy", None), P(), P(), P(), P(), P(), P(), P(), P(), P(), P())
    return jax.shard_map(
        body, mesh=mesh, in_specs=placed, out_specs=P(None, "xy", "gz", None), check_vma=False
    )
```

```python
import functools

import jax
import jax.numpy as jnp
from jax import lax
from jax.experimental import pallas as pl
from jax.experimental.pallas import tpu as pltpu
from jax.sharding import PartitionSpec as P

T2, T3, BIAS = 1024, 2048, 2816
HALO = 24
VMEM = pl.BlockSpec(memory_space=pltpu.VMEM)
F32 = jnp.float32
BF16 = jnp.bfloat16


def unrolled(count, step):
    for i in range(count):
        step(i, 0)


def lane_iota(shape):
    return lax.broadcasted_iota(jnp.int32, shape, len(shape) - 1)


def shift_rows(x, down):
    sub = lax.broadcasted_iota(jnp.int32, x.shape, 2)
    if down:
        rolled = pltpu.roll(x, 1, 2)
        other = jnp.concatenate([rolled[:, -1:], rolled[:, :-1]], axis=1)
        return jnp.where(sub == 0, other, rolled)
    rolled = pltpu.roll(x, 7, 2)
    other = jnp.concatenate([rolled[:, 1:], rolled[:, :1]], axis=1)
    return jnp.where(sub == 7, other, rolled)


def tile_lanes(ref, row):
    x = ref[row : row + 1, :]
    return x + pltpu.roll(x, 32, 1) + pltpu.roll(x, 64, 1) + pltpu.roll(x, 96, 1)


def weight_kernel(w1, b1, w2, b2, w3, b3, banded, small):
    small[...] = jnp.zeros_like(small)
    for ky in range(3):
        small[3 * ky : 3 * ky + 3, 0:32] = w1[ky].astype(F32)
    small[9:10, 0:32] = b1[...]
    small[10:11, 0:64] = b2[...]
    tap = []
    for i in range(10):
        x = tile_lanes(small, i)
        tap.append(jnp.concatenate([x, x], axis=1))
    banded[...] = jnp.zeros_like(banded)
    x = small[10:11, :]
    x = x + pltpu.roll(x, 64, 1)
    row = lax.broadcasted_iota(jnp.int32, (16, 256), 0)
    rest = jnp.where(row < 3, tap[9], jnp.where(row < 6, jnp.concatenate([x, x], axis=1), jnp.concatenate([b3[...]] * 2, axis=1)))
    high = rest.astype(BF16).astype(F32)
    mid = (rest - high).astype(BF16).astype(F32)
    low = rest - high - mid
    banded[BIAS : BIAS + 16, :] = jnp.where(row % 3 == 0, high, jnp.where(row % 3 == 1, mid, low)).astype(BF16)
    gap = lax.broadcasted_iota(jnp.int32, (32, 256), 0) - 2 * (lane_iota((32, 256)) // 32)
    for ky in range(3):
        for dx in range(2):
            band = jnp.zeros((32, 256), F32)
            for kx in range(3):
                band = jnp.where(gap == dx + kx, tap[3 * ky + kx], band)
            band = band.astype(BF16)
            for dy in range(2):
                phase = 2 * dy + dx
                at = 256 * phase + 64 * (ky + dy)
                banded[at : at + 32, :] = band

    for ky in range(3):
        for kx in range(3):
            w = w2[ky, kx]
            for dy in range(2):
                for dx in range(2):
                    r, c = ky + dy, kx + dx
                    lanes = slice(128 * dy + 64 * dx, 128 * dy + 64 * dx + 64)
                    at = T2 + 128 * r + 32 * c
                    banded[at : at + 32, lanes] = w
                    at = T2 + 512 + 128 * r + 32 * ((c + 2) % 4)
                    banded[at : at + 32, lanes] = w
            w = w3[ky, kx]
            for dx in range(2):
                at = T3 + 256 * ky + 64 * (kx + dx)
                banded[at : at + 64, 128 * dx : 128 * dx + 128] = w


def plane_kernel(
    cfg, swap_a, raw, swap_b, banded, out,
    rs, dd, ff, ppe, ppo,
):
    zl, rows, width, dests, vb = cfg
    third_rows = rows // 8
    tiles = third_rows // 8 + 1
    period = tiles * 8
    m = zl * period
    groups = width // 16 + 1
    first = lax.axis_index("xy") == 0
    last = lax.axis_index("xy") == lax.axis_size("xy") - 1
    even = lax.axis_index("xy") % 2 == 0
    sub8 = lax.broadcasted_iota(jnp.int32, (1, 1, 8, 128), 2)
    keep = jnp.where(sub8 < 4, jnp.where(last, 0.0, 1.0), jnp.where(first, 0.0, 1.0))

    def masked(x):
        n, lanes = x.shape
        x = x.reshape(n // period, tiles, 8, lanes)
        k = jnp.concatenate([keep] * (lanes // 128), axis=3)
        return jnp.concatenate([x[:, :-1], x[:, -1:] * k], axis=1)

    for z in range(zl):
        a32, b32 = swap_a[z].astype(F32), swap_b[z].astype(F32)
        lo32, hi32 = jnp.where(even, b32, a32), jnp.where(even, a32, b32)
        raw32 = raw[z].astype(F32)
        end = 8 + 8 * period
        rs[z, 0] = jnp.zeros((end + 8, 128), F32)
        rs[z, width // 128 + 1] = jnp.zeros((end + 8, 128), F32)
        for t in range(width // 128):
            cols = slice(128 * t, 128 * t + 128)
            rs[z, t + 1, 0:8] = lo32[HALO - 8 :, cols]
            rs[z, t + 1, 8 : 8 + rows] = raw32[:, cols]
            rs[z, t + 1, 8 + rows : 8 + rows + HALO] = hi32[:, cols]
            rs[z, t + 1, 8 + rows + HALO : end - HALO] = jnp.zeros((8 * period - rows - 2 * HALO, 128), F32)
            rs[z, t + 1, end - HALO : end] = lo32[:, cols]
            rs[z, t + 1, end : end + 8] = raw32[0:8, cols]

    lane = lane_iota((period, 128))
    for g in range(groups):
        start = 16 * g + 125
        t, s = start // 128, start % 128
        left = 128 - s
        for z in range(zl):
            for k in range(5):
                def piece(phase, tile, amount):
                    x = rs[z, tile, pl.ds(8 + phase, period, stride=8), :]
                    return pltpu.roll(x, amount % 128, 1)

                a = piece(2 * k - 1, t, -s)
                b = piece(2 * k, t, 64 - s)
                if left < 18:
                    a = jnp.where(lane < left, a, piece(2 * k - 1, t + 1, -s))
                    b = jnp.where(lane < 64 + left, b, piece(2 * k, t + 1, 64 - s))
                dd[k, g * m + z * period : g * m + z * period + period, :] = jnp.where(lane < 64, a, b).astype(BF16)

    bias = [sum(banded[BIAS + 3 * i + j : BIAS + 3 * i + j + 1, :].astype(F32) for j in range(3)) for i in range(3)]
    bias1, bias2, bias3 = bias[0], bias[1][:, :128], bias[2][:, :128]

    chunk = 11 if groups % 11 == 0 else 1
    n = chunk * m
    for m1 in range(4):
        def level1(c, _, m1=m1):
            at = c * n
            x = jnp.concatenate([dd[m1, pl.ds(at, n), :], dd[m1 + 1, pl.ds(at, n), :]], axis=1)
            acc = None
            for phase in range(4):
                y = jnp.dot(x, banded[256 * phase : 256 * phase + 256, :], preferred_element_type=F32)
                acc = y if acc is None else jnp.maximum(acc, y)
            y = masked(jnp.maximum(acc + bias1, 0.0))
            row = m + c * n
            ff[m1 + 1, pl.ds(row, n), :] = y.reshape(n, 256).astype(BF16)
            if m1 == 0:
                ff[5, pl.ds(row, n), :] = shift_rows(y, False).reshape(n, 256).astype(BF16)
            if m1 == 3:
                ff[0, pl.ds(row, n), :] = shift_rows(y, True).reshape(n, 256).astype(BF16)
            return 0

        unrolled(groups // chunk, level1)
    for f in range(6):
        ff[f, 0:m, :] = jnp.zeros((m, 256), BF16)
        x = ff[f, m : 2 * m, 0:128].astype(F32)
        ff[f, m : 2 * m, 0:128] = jnp.where(lane_iota((m, 128)) < 32, 0.0, x).astype(BF16)
        x = ff[f, groups * m : (groups + 1) * m, 0:128].astype(F32)
        ff[f, groups * m : (groups + 1) * m, 0:128] = jnp.where(lane_iota((m, 128)) < 32, x, 0.0).astype(BF16)
        ff[f, groups * m : (groups + 1) * m, 128:256] = jnp.zeros((m, 128), BF16)

    def half(f, at, n, lanes):
        return ff[f, pl.ds(at, n), lanes : lanes + 128]

    def swapped(f, at_low, low, at_high, high, n):
        mask = lane_iota((n, 128)) < 64
        return jnp.where(mask, half(f, at_low, n, low), half(f, at_high, n, high))

    def level2(m2, at, n, even):
        low, high = [], []
        for r in range(4):
            f = 2 * m2 + r
            if even:
                low.append(swapped(f, at, 0, at - m, 128, n))
                high.append(half(f, at, n, 0))
            else:
                low.append(swapped(f, at, 128, at, 0, n))
                high.append(half(f, at, n, 128))
        low = jnp.dot(jnp.concatenate(low, axis=1), banded[T2 + 512 : T2 + 1024, :], preferred_element_type=F32)
        high = jnp.dot(jnp.concatenate(high, axis=1), banded[T2 : T2 + 512, :], preferred_element_type=F32)
        low = jnp.maximum(low[:, :128], low[:, 128:])
        high = jnp.maximum(high[:, :128], high[:, 128:])
        mask = lane_iota((n, 128)) < 64
        y = jnp.maximum(jnp.where(mask, low, high), pltpu.roll(jnp.where(mask, high, low), 64, 1))
        return masked(jnp.maximum(y + bias2, 0.0))

    for even, pp, count in ((True, ppe, groups), (False, ppo, groups - 1)):
        chunk = 11 if count % 11 == 0 else 8 if count % 8 == 0 else 1
        n = chunk * m
        for m2 in range(2):
            def step(c, _, m2=m2, even=even, pp=pp, n=n):
                at = c * n
                y = level2(m2, at + m, n, even)
                pp[m2 + 1, pl.ds(at, n), :] = y.reshape(n, 128).astype(BF16)
                if m2 == 0:
                    pp[3, pl.ds(at, n), :] = shift_rows(y, False).reshape(n, 128).astype(BF16)
                else:
                    pp[0, pl.ds(at, n), :] = shift_rows(y, True).reshape(n, 128).astype(BF16)
                return 0

            unrolled(count // chunk, step)
    for s in range(4):
        x = ppe[s, 0:m, :].astype(F32)
        ppe[s, 0:m, :] = jnp.where(lane_iota((m, 128)) < 64, 0.0, x).astype(BF16)
        at = (groups - 1) * m
        x = ppe[s, at : at + m, :].astype(F32)
        ppe[s, at : at + m, :] = jnp.where(lane_iota((m, 128)) < 64, x, 0.0).astype(BF16)

    def level3(at, n, odd):
        acc = None
        for dy in range(2):
            x = []
            for r in range(3):
                here = pl.ds(at, n)
                after = pl.ds(at + m, n)
                x += [ppo[dy + r, here, :], ppe[dy + r, after, :]] if odd else [ppe[dy + r, here, :], ppo[dy + r, here, :]]
            y = jnp.dot(jnp.concatenate(x, axis=1), banded[T3 : T3 + 768, :], preferred_element_type=F32)
            y = jnp.maximum(y[:, :128], y[:, 128:])
            acc = y if acc is None else jnp.maximum(acc, y)
        y = masked(jnp.maximum(acc + bias3, 0.0))
        return y.reshape(n // m, zl, tiles, 8, 128)

    zero = jnp.zeros((2 * (tiles - 1) + 1, zl * 8, 128), BF16)
    out[0, 0] = zero
    out[dests - 1, vb + 1] = zero
    chunk = 8
    n = chunk * m
    for c in range((groups - 1) // chunk):
        ys = [level3(c * n, n, odd) for odd in (False, True)]
        a, b = [y[:, :, tiles - 1].reshape(chunk * zl, 8, 128) for y in ys]
        sub = lax.broadcasted_iota(jnp.int32, a.shape, 1)
        edge = jnp.where(sub < 4, pltpu.roll(a, 2, 1), pltpu.roll(b, 6, 1))
        edge = edge.reshape(chunk, zl * 8, 128).astype(BF16)
        mains = [y[:, :, i].reshape(chunk, zl * 8, 128).astype(BF16) for y in ys for i in range(tiles - 1)]
        for w in range(chunk):
            v = c * chunk + w
            for d in range(dests):
                at = v - (vb * d - 1)
                if 0 <= at < vb + 2:
                    for i, part in enumerate(mains + [edge]):
                        out[d, at, i] = part[w]


def cube_kernel(cfg, *refs):
    sources, zl, third_rows, vb, in_chan, mid_chan, out_chan, flip = cfg
    near, far = refs[: sources // 2], refs[sources // 2 : sources]
    wa, ba, wb, bb, out, a3, b3 = refs[sources:]
    me = lax.axis_index("gz")
    depth = sources * zl
    xs = 2 * vb
    tiles = third_rows // 8

    rows = 8 * depth
    shape = (rows, rows)
    to = lax.broadcasted_iota(jnp.int32, shape, 0)
    at = lax.broadcasted_iota(jnp.int32, shape, 1)
    k_to, z_to = to // depth, to % depth
    k_at, z_at = at % 8, ((at // (8 * zl)) ^ me) * zl + (at // 8) % zl
    gather = jnp.concatenate(
        [jnp.where((k_to == k_at) & (z_at == z_to + dz), 1.0, 0.0).astype(BF16) for dz in (-1, 0, 1)], axis=0
    )
    parts = 2 * tiles + 1
    for vl in range(vb + 2):
        for c in range(parts):
            x = jnp.concatenate(
                [part for k in range(sources // 2) for part in (near[k][(me % 2) * vb + vl, c], far[k][vl, c])], axis=0
            )
            y = jnp.dot(gather, x, preferred_element_type=F32).astype(BF16).reshape(3, 8, depth, in_chan)
            for dz in range(3):
                lanes = slice(dz * in_chan, (dz + 1) * in_chan)
                if c < 2 * tiles:
                    x_at, y_at = 2 * vl + c // tiles, 2 + 8 * (c % tiles)
                    a3[y_at : y_at + 8, x_at, :, lanes] = y[dz]
                else:
                    for side in range(2):
                        a3[0:2, 2 * vl + side, :, lanes] = y[dz, 4 * side : 4 * side + 2]
                        a3[third_rows + 2 : third_rows + 4, 2 * vl + side, :, lanes] = y[dz, 4 * side + 2 : 4 * side + 4]

    taps = [(ky, kx) for ky in range(3) for kx in range(3)]
    mid_x = xs + 2
    mid_rows = third_rows + 2
    step_rows = 9 if mid_rows % 9 == 0 else 1

    def iso_a(c, _):
        y0 = c * step_rows
        n = step_rows * mid_x * depth
        x = jnp.concatenate(
            [a3[pl.ds(y0 + ky, step_rows), kx : kx + mid_x].reshape(n, 3 * in_chan) for ky, kx in taps], axis=1
        )
        w = jnp.concatenate([wa[dz, ky, kx] for ky, kx in taps for dz in range(3)], axis=0)
        y = jnp.dot(x, w, preferred_element_type=F32)
        y = jnp.maximum(y + ba[...], 0.0)
        here = (step_rows, mid_x, depth, mid_chan)
        b3[pl.ds(y0, step_rows), :, :, mid_chan : 2 * mid_chan] = y.reshape(here).astype(BF16)
        y = y.reshape(step_rows * mid_x, depth // 8, 8, mid_chan)
        sub = lax.broadcasted_iota(jnp.int32, y.shape, 2)
        none = jnp.zeros_like(y[:, :1])
        rolled = pltpu.roll(y, 1, 2)
        other = jnp.concatenate([none, rolled[:, :-1]], axis=1)
        down = jnp.where(sub == 0, other, rolled)
        b3[pl.ds(y0, step_rows), :, :, 0:mid_chan] = down.reshape(here).astype(BF16)
        rolled = pltpu.roll(y, 7, 2)
        other = jnp.concatenate([rolled[:, 1:], none], axis=1)
        up = jnp.where(sub == 7, other, rolled)
        b3[pl.ds(y0, step_rows), :, :, 2 * mid_chan : 3 * mid_chan] = up.reshape(here).astype(BF16)
        return 0

    lax.fori_loop(0, mid_rows // step_rows, iso_a, 0)

    row, col = lax.axis_index("xy"), lax.axis_index("gz")

    @pl.when(row == 0)
    def _():
        b3[0] = jnp.zeros(b3.shape[1:], BF16)

    @pl.when(row == lax.axis_size("xy") - 1)
    def _():
        b3[mid_rows - 1] = jnp.zeros(b3.shape[1:], BF16)

    @pl.when(col == 0)
    def _():
        b3[:, 0] = jnp.zeros((mid_rows,) + b3.shape[2:], BF16)

    @pl.when(col == lax.axis_size("gz") - 1)
    def _():
        b3[:, mid_x - 1] = jnp.zeros((mid_rows,) + b3.shape[2:], BF16)

    if flip:
        n = xs * depth
        to = lax.broadcasted_iota(jnp.int32, (n, n), 0)
        at = lax.broadcasted_iota(jnp.int32, (n, n), 1)
        turn = jnp.where((to // xs == at % depth) & (to % xs == at // depth), 1.0, 0.0).astype(BF16)
    out_rows = 8

    def iso_b(c, _):
        y0 = c * out_rows
        n = out_rows * xs * depth
        x = jnp.concatenate(
            [b3[pl.ds(y0 + ky, out_rows), kx : kx + xs].reshape(n, 3 * mid_chan) for ky, kx in taps], axis=1
        )
        w = jnp.concatenate([wb[dz, ky, kx] for ky, kx in taps for dz in range(3)], axis=0)
        y = jnp.dot(x, w, preferred_element_type=F32)
        y = jnp.maximum(y + bb[...], 0.0).astype(BF16)
        if flip:
            y = y.reshape(out_rows, xs * depth, out_chan)
            for i in range(out_rows):
                t = jnp.dot(turn, y[i], preferred_element_type=F32).astype(BF16)
                out[:, y0 + i] = t.reshape(depth, xs, out_chan)
        else:
            out[pl.ds(y0, out_rows)] = y.reshape(out_rows, xs, depth, out_chan)
        return 0

    lax.fori_loop(0, third_rows // out_rows, iso_b, 0)


def body(
    raw_volume,
    weight_first,
    bias_first,
    weight_second,
    bias_second,
    weight_third,
    bias_third,
    weight_iso_a,
    bias_iso_a,
    weight_iso_b,
    bias_iso_b,
):
    zl, rows, width = raw_volume.shape
    dests = lax.axis_size("gz")
    depth = zl * dests
    third_rows = rows // 8
    vb = width // 8 // dests // 2
    count = lax.axis_size("xy")
    even = lax.axis_index("xy") % 2 == 0

    def swap(start, pairs):
        edge = lax.dynamic_slice_in_dim(raw_volume, start, HALO, axis=1)
        return lax.ppermute(edge, "xy", [(i, i + 1) for i in pairs] + [(i + 1, i) for i in pairs])

    first = swap(jnp.where(even, rows - HALO, 0), range(0, count - 1, 2))
    second = swap(jnp.where(even, 0, rows - HALO), range(1, count - 1, 2))

    period = third_rows + 8
    m = zl * period
    groups = width // 16 + 1
    parts = 2 * (third_rows // 8) + 1
    banded = pl.pallas_call(
        weight_kernel,
        out_shape=jax.ShapeDtypeStruct((BIAS + 16, 256), BF16),
        in_specs=[VMEM] * 6,
        out_specs=VMEM,
        scratch_shapes=[pltpu.VMEM((16, 128), F32)],
        compiler_params=pltpu.CompilerParams(vmem_limit_bytes=60 << 20),
        cost_estimate=pl.CostEstimate(flops=2000000000, bytes_accessed=2000000, transcendentals=0),
        name="weights",
    )(
        jnp.transpose(weight_first, (1, 2, 3, 0))[0], bias_first[None],
        jnp.transpose(weight_second, (2, 3, 1, 0)), bias_second[None],
        jnp.transpose(weight_third, (2, 3, 1, 0)), bias_third[None],
    )
    chips = dests // 2
    send = pl.pallas_call(
        functools.partial(plane_kernel, (zl, rows, width, chips, 2 * vb)),
        out_shape=jax.ShapeDtypeStruct((chips, 2 * vb + 2, parts, zl * 8, 128), BF16),
        in_specs=[VMEM] * 4,
        out_specs=VMEM,
        scratch_shapes=[
            pltpu.VMEM((zl, width // 128 + 2, 8 * period + 16, 128), F32),
            pltpu.VMEM((5, groups * m, 128), BF16),
            pltpu.VMEM((6, (groups + 1) * m, 256), BF16),
            pltpu.VMEM((4, groups * m, 128), BF16),
            pltpu.VMEM((4, (groups - 1) * m, 128), BF16),
        ],
        compiler_params=pltpu.CompilerParams(vmem_limit_bytes=20 << 20),
        name="planes",
    )(first, raw_volume, second, banded)
    me = lax.axis_index("gz")
    other = (1 - me % 2) * vb
    near, far = [], []
    for k in range(chips):
        block = lax.dynamic_index_in_dim(send, (me // 2) ^ k, 0, keepdims=False)
        if k:
            block = lax.ppermute(block, "gz", [(i, i ^ (2 * k)) for i in range(dests)])
        near.append(block)
        window = lax.dynamic_slice_in_dim(block, other, vb + 2, axis=0)
        far.append(lax.ppermute(window, "gz", [(i, i ^ 1) for i in range(dests)]))

    xs = 2 * vb
    in_chan, mid_chan = weight_iso_a.shape[3:]
    out_chan = weight_iso_b.shape[4]
    flip = xs % 8 == 0
    shape = (depth, third_rows, xs, out_chan) if flip else (third_rows, xs, depth, out_chan)
    out = pl.pallas_call(
        functools.partial(cube_kernel, (dests, zl, third_rows, vb, in_chan, mid_chan, out_chan, flip)),
        out_shape=jax.ShapeDtypeStruct(shape, BF16),
        in_specs=[VMEM] * (dests + 4),
        out_specs=VMEM,
        scratch_shapes=[
            pltpu.VMEM((third_rows + 4, xs + 4, depth, 3 * in_chan), BF16),
            pltpu.VMEM((third_rows + 2, xs + 2, depth, 3 * mid_chan), BF16),
        ],
        compiler_params=pltpu.CompilerParams(vmem_limit_bytes=(20 if depth <= 16 else 48) << 20),
        name="cubes",
    )(*near, *far, weight_iso_a, bias_iso_a[None], weight_iso_b, bias_iso_b[None])
    return out if flip else jnp.transpose(out, (2, 0, 1, 3))


def solution(mesh):
    placed = (P("gz", "xy", None), P(), P(), P(), P(), P(), P(), P(), P(), P(), P())
    return jax.shard_map(
        body, mesh=mesh, in_specs=placed, out_specs=P(None, "xy", "gz", None), check_vma=False
    )
```

```python
import functools

import jax
import jax.numpy as jnp
from jax import lax
from jax.experimental import pallas as pl
from jax.experimental.pallas import tpu as pltpu
from jax.sharding import PartitionSpec as P

T2, T3, BIAS = 1024, 2048, 2816
HALO = 24
VMEM = pl.BlockSpec(memory_space=pltpu.VMEM)
F32 = jnp.float32
BF16 = jnp.bfloat16


def unrolled(count, step):
    for i in range(count):
        step(i, 0)


def lane_iota(shape):
    return lax.broadcasted_iota(jnp.int32, shape, len(shape) - 1)


def shift_rows(x, down):
    sub = lax.broadcasted_iota(jnp.int32, x.shape, 2)
    if down:
        rolled = pltpu.roll(x, 1, 2)
        other = jnp.concatenate([rolled[:, -1:], rolled[:, :-1]], axis=1)
        return jnp.where(sub == 0, other, rolled)
    rolled = pltpu.roll(x, 7, 2)
    other = jnp.concatenate([rolled[:, 1:], rolled[:, :1]], axis=1)
    return jnp.where(sub == 7, other, rolled)


def tile_lanes(ref, row):
    x = ref[row : row + 1, :]
    return x + pltpu.roll(x, 32, 1) + pltpu.roll(x, 64, 1) + pltpu.roll(x, 96, 1)


def weight_kernel(w1, b1, w2, b2, w3, b3, banded, small):
    small[...] = jnp.zeros_like(small)
    for ky in range(3):
        small[3 * ky : 3 * ky + 3, 0:32] = w1[ky].astype(F32)
    small[9:10, 0:32] = b1[...]
    small[10:11, 0:64] = b2[...]
    tap = []
    for i in range(10):
        x = tile_lanes(small, i)
        tap.append(jnp.concatenate([x, x], axis=1))
    banded[...] = jnp.zeros_like(banded)
    x = small[10:11, :]
    x = x + pltpu.roll(x, 64, 1)
    row = lax.broadcasted_iota(jnp.int32, (16, 256), 0)
    rest = jnp.where(row < 3, tap[9], jnp.where(row < 6, jnp.concatenate([x, x], axis=1), jnp.concatenate([b3[...]] * 2, axis=1)))
    high = rest.astype(BF16).astype(F32)
    mid = (rest - high).astype(BF16).astype(F32)
    low = rest - high - mid
    banded[BIAS : BIAS + 16, :] = jnp.where(row % 3 == 0, high, jnp.where(row % 3 == 1, mid, low)).astype(BF16)
    gap = lax.broadcasted_iota(jnp.int32, (32, 256), 0) - 2 * (lane_iota((32, 256)) // 32)
    for ky in range(3):
        for dx in range(2):
            band = jnp.zeros((32, 256), F32)
            for kx in range(3):
                band = jnp.where(gap == dx + kx, tap[3 * ky + kx], band)
            band = band.astype(BF16)
            for dy in range(2):
                phase = 2 * dy + dx
                at = 256 * phase + 64 * (ky + dy)
                banded[at : at + 32, :] = band

    for ky in range(3):
        for kx in range(3):
            w = w2[ky, kx]
            for dy in range(2):
                for dx in range(2):
                    r, c = ky + dy, kx + dx
                    lanes = slice(128 * dy + 64 * dx, 128 * dy + 64 * dx + 64)
                    at = T2 + 128 * r + 32 * c
                    banded[at : at + 32, lanes] = w
                    at = T2 + 512 + 128 * r + 32 * ((c + 2) % 4)
                    banded[at : at + 32, lanes] = w
            w = w3[ky, kx]
            for dx in range(2):
                at = T3 + 256 * ky + 64 * (kx + dx)
                banded[at : at + 64, 128 * dx : 128 * dx + 128] = w


def plane_kernel(
    cfg, swap_a, raw, swap_b, banded, out,
    rs, dd, ff, ppe, ppo,
):
    zl, rows, width, dests, vb = cfg
    third_rows = rows // 8
    tiles = third_rows // 8 + 1
    period = tiles * 8
    m = zl * period
    groups = width // 16 + 1
    first = lax.axis_index("xy") == 0
    last = lax.axis_index("xy") == lax.axis_size("xy") - 1
    even = lax.axis_index("xy") % 2 == 0
    sub8 = lax.broadcasted_iota(jnp.int32, (1, 1, 8, 128), 2)
    keep = jnp.where(sub8 < 4, jnp.where(last, 0.0, 1.0), jnp.where(first, 0.0, 1.0))

    def masked(x):
        n, lanes = x.shape
        x = x.reshape(n // period, tiles, 8, lanes)
        k = jnp.concatenate([keep] * (lanes // 128), axis=3)
        return jnp.concatenate([x[:, :-1], x[:, -1:] * k], axis=1)

    for z in range(zl):
        a32, b32 = swap_a[z].astype(F32), swap_b[z].astype(F32)
        lo32, hi32 = jnp.where(even, b32, a32), jnp.where(even, a32, b32)
        raw32 = raw[z].astype(F32)
        end = 8 + 8 * period
        rs[z, 0] = jnp.zeros((end + 8, 128), F32)
        rs[z, width // 128 + 1] = jnp.zeros((end + 8, 128), F32)
        for t in range(width // 128):
            cols = slice(128 * t, 128 * t + 128)
            rs[z, t + 1, 0:8] = lo32[HALO - 8 :, cols]
            rs[z, t + 1, 8 : 8 + rows] = raw32[:, cols]
            rs[z, t + 1, 8 + rows : 8 + rows + HALO] = hi32[:, cols]
            rs[z, t + 1, 8 + rows + HALO : end - HALO] = jnp.zeros((8 * period - rows - 2 * HALO, 128), F32)
            rs[z, t + 1, end - HALO : end] = lo32[:, cols]
            rs[z, t + 1, end : end + 8] = raw32[0:8, cols]

    lane = lane_iota((period, 128))
    for g in range(groups):
        start = 16 * g + 125
        t, s = start // 128, start % 128
        left = 128 - s
        for z in range(zl):
            for k in range(5):
                def piece(phase, tile, amount):
                    x = rs[z, tile, pl.ds(8 + phase, period, stride=8), :]
                    return pltpu.roll(x, amount % 128, 1)

                a = piece(2 * k - 1, t, -s)
                b = piece(2 * k, t, 64 - s)
                if left < 18:
                    a = jnp.where(lane < left, a, piece(2 * k - 1, t + 1, -s))
                    b = jnp.where(lane < 64 + left, b, piece(2 * k, t + 1, 64 - s))
                dd[k, g * m + z * period : g * m + z * period + period, :] = jnp.where(lane < 64, a, b).astype(BF16)

    bias = [sum(banded[BIAS + 3 * i + j : BIAS + 3 * i + j + 1, :].astype(F32) for j in range(3)) for i in range(3)]
    bias1, bias2, bias3 = bias[0], bias[1][:, :128], bias[2][:, :128]

    chunk = 11 if groups % 11 == 0 else 1
    n = chunk * m
    for m1 in range(4):
        def level1(c, _, m1=m1):
            at = c * n
            x = jnp.concatenate([dd[m1, pl.ds(at, n), :], dd[m1 + 1, pl.ds(at, n), :]], axis=1)
            acc = None
            for phase in range(4):
                y = jnp.dot(x, banded[256 * phase : 256 * phase + 256, :], preferred_element_type=F32)
                acc = y if acc is None else jnp.maximum(acc, y)
            y = masked(jnp.maximum(acc + bias1, 0.0))
            row = m + c * n
            ff[m1 + 1, pl.ds(row, n), :] = y.reshape(n, 256).astype(BF16)
            if m1 == 0:
                ff[5, pl.ds(row, n), :] = shift_rows(y, False).reshape(n, 256).astype(BF16)
            if m1 == 3:
                ff[0, pl.ds(row, n), :] = shift_rows(y, True).reshape(n, 256).astype(BF16)
            return 0

        unrolled(groups // chunk, level1)
    for f in range(6):
        ff[f, 0:m, :] = jnp.zeros((m, 256), BF16)
        x = ff[f, m : 2 * m, 0:128].astype(F32)
        ff[f, m : 2 * m, 0:128] = jnp.where(lane_iota((m, 128)) < 32, 0.0, x).astype(BF16)
        x = ff[f, groups * m : (groups + 1) * m, 0:128].astype(F32)
        ff[f, groups * m : (groups + 1) * m, 0:128] = jnp.where(lane_iota((m, 128)) < 32, x, 0.0).astype(BF16)
        ff[f, groups * m : (groups + 1) * m, 128:256] = jnp.zeros((m, 128), BF16)

    def half(f, at, n, lanes):
        return ff[f, pl.ds(at, n), lanes : lanes + 128]

    def swapped(f, at_low, low, at_high, high, n):
        mask = lane_iota((n, 128)) < 64
        return jnp.where(mask, half(f, at_low, n, low), half(f, at_high, n, high))

    def level2(m2, at, n, even):
        low, high = [], []
        for r in range(4):
            f = 2 * m2 + r
            if even:
                low.append(swapped(f, at, 0, at - m, 128, n))
                high.append(half(f, at, n, 0))
            else:
                low.append(swapped(f, at, 128, at, 0, n))
                high.append(half(f, at, n, 128))
        low = jnp.dot(jnp.concatenate(low, axis=1), banded[T2 + 512 : T2 + 1024, :], preferred_element_type=F32)
        high = jnp.dot(jnp.concatenate(high, axis=1), banded[T2 : T2 + 512, :], preferred_element_type=F32)
        low = jnp.maximum(low[:, :128], low[:, 128:])
        high = jnp.maximum(high[:, :128], high[:, 128:])
        mask = lane_iota((n, 128)) < 64
        y = jnp.maximum(jnp.where(mask, low, high), pltpu.roll(jnp.where(mask, high, low), 64, 1))
        return masked(jnp.maximum(y + bias2, 0.0))

    for even, pp, count in ((True, ppe, groups), (False, ppo, groups - 1)):
        chunk = 11 if count % 11 == 0 else 8 if count % 8 == 0 else 1
        n = chunk * m
        for m2 in range(2):
            def step(c, _, m2=m2, even=even, pp=pp, n=n):
                at = c * n
                y = level2(m2, at + m, n, even)
                pp[m2 + 1, pl.ds(at, n), :] = y.reshape(n, 128).astype(BF16)
                if m2 == 0:
                    pp[3, pl.ds(at, n), :] = shift_rows(y, False).reshape(n, 128).astype(BF16)
                else:
                    pp[0, pl.ds(at, n), :] = shift_rows(y, True).reshape(n, 128).astype(BF16)
                return 0

            unrolled(count // chunk, step)
    for s in range(4):
        x = ppe[s, 0:m, :].astype(F32)
        ppe[s, 0:m, :] = jnp.where(lane_iota((m, 128)) < 64, 0.0, x).astype(BF16)
        at = (groups - 1) * m
        x = ppe[s, at : at + m, :].astype(F32)
        ppe[s, at : at + m, :] = jnp.where(lane_iota((m, 128)) < 64, x, 0.0).astype(BF16)

    def level3(at, n, odd):
        acc = None
        for dy in range(2):
            x = []
            for r in range(3):
                here = pl.ds(at, n)
                after = pl.ds(at + m, n)
                x += [ppo[dy + r, here, :], ppe[dy + r, after, :]] if odd else [ppe[dy + r, here, :], ppo[dy + r, here, :]]
            y = jnp.dot(jnp.concatenate(x, axis=1), banded[T3 : T3 + 768, :], preferred_element_type=F32)
            y = jnp.maximum(y[:, :128], y[:, 128:])
            acc = y if acc is None else jnp.maximum(acc, y)
        y = masked(jnp.maximum(acc + bias3, 0.0))
        return y.reshape(n // m, zl, tiles, 8, 128)

    zero = jnp.zeros((2 * (tiles - 1) + 1, zl * 8, 128), BF16)
    out[0, 0] = zero
    out[dests - 1, vb + 1] = zero
    chunk = 8
    n = chunk * m
    for c in range((groups - 1) // chunk):
        ys = [level3(c * n, n, odd) for odd in (False, True)]
        a, b = [y[:, :, tiles - 1].reshape(chunk * zl, 8, 128) for y in ys]
        sub = lax.broadcasted_iota(jnp.int32, a.shape, 1)
        edge = jnp.where(sub < 4, pltpu.roll(a, 2, 1), pltpu.roll(b, 6, 1))
        edge = edge.reshape(chunk, zl * 8, 128).astype(BF16)
        mains = [y[:, :, i].reshape(chunk, zl * 8, 128).astype(BF16) for y in ys for i in range(tiles - 1)]
        for w in range(chunk):
            v = c * chunk + w
            for d in range(dests):
                at = v - (vb * d - 1)
                if 0 <= at < vb + 2:
                    for i, part in enumerate(mains + [edge]):
                        out[d, at, i] = part[w]


def filter_kernel(send, w, u, window):
    me = lax.axis_index("gz")
    pairs = window.shape[0]
    window[...] = send[me // 2, pl.ds((1 - me % 2) * (pairs - 2), pairs)]
    chan = w.shape[3]
    for kx in range(3):
        for dz in range(3):
            at = slice((3 * kx + dz) * chan, (3 * kx + dz + 1) * chan)
            g0, g1, g2 = (w[dz, ky, kx].astype(F32) for ky in range(3))
            outer, inner = 0.5 * (g0 + g2), 0.5 * g1
            u[0, at] = w[dz, 0, kx]
            u[1, at] = (outer + inner).astype(BF16)
            u[2, at] = (outer - inner).astype(BF16)
            u[3, at] = w[dz, 2, kx]


def four_rows(x):
    x = x.reshape((x.shape[0] // 2, 2) + x.shape[1:])
    even, odd = x[:, 0], x[:, 1]
    return (even[:-1] - even[1:], odd[:-1] + even[1:], even[1:] - odd[:-1], odd[:-1] - odd[1:])


def cube_kernel(cfg, *refs):
    sources, zl, third_rows, vb, in_chan, mid_chan, out_chan, flip = cfg
    near, far = refs[: sources // 2], refs[sources // 2 : sources]
    wa, ba, ub, bb, out, a3, mid, vm, ms = refs[sources:]
    me = lax.axis_index("gz")
    depth = sources * zl
    xs = 2 * vb
    tiles = third_rows // 8

    rows = 8 * depth
    shape = (rows, rows)
    to = lax.broadcasted_iota(jnp.int32, shape, 0)
    at = lax.broadcasted_iota(jnp.int32, shape, 1)
    k_to, z_to = to // depth, to % depth
    k_at, z_at = at % 8, ((at // (8 * zl)) ^ me) * zl + (at // 8) % zl
    gather = jnp.concatenate(
        [jnp.where((k_to == k_at) & (z_at == z_to + dz), 1.0, 0.0).astype(BF16) for dz in (-1, 0, 1)], axis=0
    )
    parts = 2 * tiles + 1
    for vl in range(vb + 2):
        for c in range(parts):
            x = jnp.concatenate(
                [part for k in range(sources // 2) for part in (near[k][(me % 2) * vb + vl, c], far[k][vl, c])], axis=0
            )
            y = jnp.dot(gather, x, preferred_element_type=F32).astype(BF16).reshape(3, 8, depth, in_chan)
            for dz in range(3):
                lanes = slice(dz * in_chan, (dz + 1) * in_chan)
                if c < 2 * tiles:
                    x_at, y_at = 2 * vl + c // tiles, 2 + 8 * (c % tiles)
                    a3[y_at : y_at + 8, x_at, :, lanes] = y[dz]
                else:
                    for side in range(2):
                        a3[0:2, 2 * vl + side, :, lanes] = y[dz, 4 * side : 4 * side + 2]
                        a3[third_rows + 2 : third_rows + 4, 2 * vl + side, :, lanes] = y[dz, 4 * side + 2 : 4 * side + 4]

    taps = [(ky, kx) for ky in range(3) for kx in range(3)]
    mid_x = xs + 2
    mid_rows = third_rows + 2
    step = 9 if mid_rows % 9 == 0 else 1

    def iso_a(c, _):
        first = c * step
        n = step * mid_x * depth
        x = jnp.concatenate([a3[pl.ds(first + ky, step), kx : kx + mid_x].reshape(n, 3 * in_chan) for ky, kx in taps], axis=1)
        w = jnp.concatenate([wa[dz, ky, kx] for ky, kx in taps for dz in range(3)], axis=0)
        y = jnp.maximum(jnp.dot(x, w, preferred_element_type=F32) + ba[...], 0.0)
        mid[pl.ds(first, step)] = y.reshape(step, mid_x, depth, mid_chan).astype(BF16)
        return 0

    lax.fori_loop(0, mid_rows // step, iso_a, 0)

    def products(v, u, first, count, breadth, chan):
        n = count * breadth * depth
        slot = (first // count) % 2
        for t in range(4):
            x = jnp.concatenate([v[t, first : first + count, kx : kx + breadth].reshape(n, 3 * chan) for kx in range(3)], axis=1)
            ms[slot, t, 0:n] = jnp.dot(x, u[t], preferred_element_type=F32)
        m1, m2 = ms[slot, 1, 0:n], ms[slot, 2, 0:n]
        return ms[slot, 0, 0:n] + (m1 + m2), (m1 - m2) - ms[slot, 3, 0:n]

    row, col = lax.axis_index("xy"), lax.axis_index("gz")

    @pl.when(row == 0)
    def _():
        mid[0] = jnp.zeros(mid.shape[1:], BF16)

    @pl.when(row == lax.axis_size("xy") - 1)
    def _():
        mid[mid_rows - 1] = jnp.zeros(mid.shape[1:], BF16)

    @pl.when(col == 0)
    def _():
        mid[:, 0] = jnp.zeros(mid.shape[:1] + mid.shape[2:], BF16)

    @pl.when(col == lax.axis_size("gz") - 1)
    def _():
        mid[:, mid_x - 1] = jnp.zeros(mid.shape[:1] + mid.shape[2:], BF16)

    pairs_b = third_rows // 2
    step = 4 if pairs_b % 4 == 0 else 1
    if flip:
        n = xs * depth
        to = lax.broadcasted_iota(jnp.int32, (n, n), 0)
        at = lax.broadcasted_iota(jnp.int32, (n, n), 1)
        turn = jnp.where((to // xs == at % depth) & (to % xs == at // depth), 1.0, 0.0).astype(BF16)
    for first in range(0, pairs_b, step):
        for x_at in range(mid_x):
            x = mid[2 * first : 2 * (first + step) + 2, x_at].astype(F32)
            for t, v in enumerate(four_rows(x)):
                here = v.shape
                vm[t, first : first + step, x_at, :, mid_chan : 2 * mid_chan] = v.astype(BF16)
                v = v.reshape(step, depth // 8, 8, mid_chan)
                sub = lax.broadcasted_iota(jnp.int32, v.shape, 2)
                none = jnp.zeros_like(v[:, :1])
                rolled = pltpu.roll(v, 1, 2)
                moved = jnp.where(sub == 0, jnp.concatenate([none, rolled[:, :-1]], axis=1), rolled)
                vm[t, first : first + step, x_at, :, 0:mid_chan] = moved.reshape(here).astype(BF16)
                rolled = pltpu.roll(v, 7, 2)
                moved = jnp.where(sub == 7, jnp.concatenate([rolled[:, 1:], none], axis=1), rolled)
                vm[t, first : first + step, x_at, :, 2 * mid_chan :] = moved.reshape(here).astype(BF16)
        for i, y in enumerate(products(vm, ub, first, step, xs, mid_chan)):
            y = jnp.maximum(y + bb[...], 0.0).astype(BF16)
            if flip:
                y = y.reshape(step, xs * depth, out_chan)
                for j in range(step):
                    t = jnp.dot(turn, y[j], preferred_element_type=F32).astype(BF16)
                    out[:, 2 * (first + j) + i] = t.reshape(depth, xs, out_chan)
            else:
                y = y.reshape(step, xs, depth, out_chan)
                for j in range(step):
                    out[2 * (first + j) + i] = y[j]


def body(
    raw_volume,
    weight_first,
    bias_first,
    weight_second,
    bias_second,
    weight_third,
    bias_third,
    weight_iso_a,
    bias_iso_a,
    weight_iso_b,
    bias_iso_b,
):
    zl, rows, width = raw_volume.shape
    dests = lax.axis_size("gz")
    depth = zl * dests
    third_rows = rows // 8
    vb = width // 8 // dests // 2
    count = lax.axis_size("xy")
    even = lax.axis_index("xy") % 2 == 0

    def swap(start, pairs):
        edge = lax.dynamic_slice_in_dim(raw_volume, start, HALO, axis=1)
        return lax.ppermute(edge, "xy", [(i, i + 1) for i in pairs] + [(i + 1, i) for i in pairs])

    first = swap(jnp.where(even, rows - HALO, 0), range(0, count - 1, 2))
    second = swap(jnp.where(even, 0, rows - HALO), range(1, count - 1, 2))

    period = third_rows + 8
    m = zl * period
    groups = width // 16 + 1
    parts = 2 * (third_rows // 8) + 1
    banded = pl.pallas_call(
        weight_kernel,
        out_shape=jax.ShapeDtypeStruct((BIAS + 16, 256), BF16),
        in_specs=[VMEM] * 6,
        out_specs=VMEM,
        scratch_shapes=[pltpu.VMEM((16, 128), F32)],
        compiler_params=pltpu.CompilerParams(vmem_limit_bytes=60 << 20),
        cost_estimate=pl.CostEstimate(flops=2000000000, bytes_accessed=2000000, transcendentals=0),
        name="weights",
    )(
        jnp.transpose(weight_first, (1, 2, 3, 0))[0], bias_first[None],
        jnp.transpose(weight_second, (2, 3, 1, 0)), bias_second[None],
        jnp.transpose(weight_third, (2, 3, 1, 0)), bias_third[None],
    )
    chips = dests // 2
    send = pl.pallas_call(
        functools.partial(plane_kernel, (zl, rows, width, chips, 2 * vb)),
        out_shape=jax.ShapeDtypeStruct((chips, 2 * vb + 2, parts, zl * 8, 128), BF16),
        in_specs=[VMEM] * 4,
        out_specs=VMEM,
        scratch_shapes=[
            pltpu.VMEM((zl, width // 128 + 2, 8 * period + 16, 128), F32),
            pltpu.VMEM((5, groups * m, 128), BF16),
            pltpu.VMEM((6, (groups + 1) * m, 256), BF16),
            pltpu.VMEM((4, groups * m, 128), BF16),
            pltpu.VMEM((4, (groups - 1) * m, 128), BF16),
        ],
        compiler_params=pltpu.CompilerParams(vmem_limit_bytes=20 << 20),
        name="planes",
    )(first, raw_volume, second, banded)
    me = lax.axis_index("gz")
    other = (1 - me % 2) * vb
    ub, own = pl.pallas_call(
        filter_kernel,
        out_shape=[
            jax.ShapeDtypeStruct((4, 9 * weight_iso_b.shape[3], weight_iso_b.shape[4]), BF16),
            jax.ShapeDtypeStruct((vb + 2,) + send.shape[2:], BF16),
        ],
        in_specs=[VMEM, VMEM],
        out_specs=[VMEM, VMEM],
        compiler_params=pltpu.CompilerParams(vmem_limit_bytes=20 << 20),
        cost_estimate=pl.CostEstimate(flops=4000000000, bytes_accessed=8000000, transcendentals=0),
        name="filters",
    )(send, weight_iso_b)
    near, far = [], []
    for k in range(chips):
        block = lax.dynamic_index_in_dim(send, (me // 2) ^ k, 0, keepdims=False)
        if k:
            block = lax.ppermute(block, "gz", [(i, i ^ (2 * k)) for i in range(dests)])
        near.append(block)
        window = lax.dynamic_slice_in_dim(block, other, vb + 2, axis=0) if k else own
        far.append(lax.ppermute(window, "gz", [(i, i ^ 1) for i in range(dests)]))

    xs = 2 * vb
    in_chan, mid_chan = weight_iso_a.shape[3:]
    out_chan = weight_iso_b.shape[4]
    flip = xs % 8 == 0
    shape = (depth, third_rows, xs, out_chan) if flip else (third_rows, xs, depth, out_chan)
    out = pl.pallas_call(
        functools.partial(cube_kernel, (dests, zl, third_rows, vb, in_chan, mid_chan, out_chan, flip)),
        out_shape=jax.ShapeDtypeStruct(shape, BF16),
        in_specs=[VMEM] * (dests + 4),
        out_specs=VMEM,
        scratch_shapes=[
            pltpu.VMEM((third_rows + 4, xs + 4, depth, 3 * in_chan), BF16),
            pltpu.VMEM((third_rows + 2, xs + 2, depth, mid_chan), BF16),
            pltpu.VMEM((4, third_rows // 2, xs + 2, depth, 3 * mid_chan), BF16),
            pltpu.VMEM((2, 4, 4 * xs * depth, mid_chan), F32),
        ],
        compiler_params=pltpu.CompilerParams(vmem_limit_bytes=(36 if depth <= 16 else 60) << 20),
        name="cubes",
    )(*near, *far, weight_iso_a, bias_iso_a[None], ub, bias_iso_b[None])
    return out if flip else jnp.transpose(out, (2, 0, 1, 3))


def solution(mesh):
    placed = (P("gz", "xy", None), P(), P(), P(), P(), P(), P(), P(), P(), P(), P())
    return jax.shard_map(
        body, mesh=mesh, in_specs=placed, out_specs=P(None, "xy", "gz", None), check_vma=False
    )
```

```python
import functools

import jax
import jax.numpy as jnp
from jax import lax
from jax.experimental import pallas as pl
from jax.experimental.pallas import tpu as pltpu
from jax.sharding import PartitionSpec as P

T2, T3, BIAS = 1024, 2048, 2816
HALO = 24
VMEM = pl.BlockSpec(memory_space=pltpu.VMEM)
F32 = jnp.float32
BF16 = jnp.bfloat16


def unrolled(count, step):
    for i in range(count):
        step(i, 0)


def lane_iota(shape):
    return lax.broadcasted_iota(jnp.int32, shape, len(shape) - 1)


def shift_rows(x, down):
    sub = lax.broadcasted_iota(jnp.int32, x.shape, 2)
    if down:
        rolled = pltpu.roll(x, 1, 2)
        other = jnp.concatenate([rolled[:, -1:], rolled[:, :-1]], axis=1)
        return jnp.where(sub == 0, other, rolled)
    rolled = pltpu.roll(x, 7, 2)
    other = jnp.concatenate([rolled[:, 1:], rolled[:, :1]], axis=1)
    return jnp.where(sub == 7, other, rolled)


def tile_lanes(ref, row):
    x = ref[row : row + 1, :]
    return x + pltpu.roll(x, 32, 1) + pltpu.roll(x, 64, 1) + pltpu.roll(x, 96, 1)


def weight_kernel(packed, biases, banded, small):
    small[0:16] = packed[864:880].astype(F32)
    small[9:11] = biases[0:2]
    tap = []
    for i in range(10):
        x = tile_lanes(small, i)
        tap.append(jnp.concatenate([x, x], axis=1))
    banded[...] = jnp.zeros_like(banded)
    x = small[10:11, :]
    x = x + pltpu.roll(x, 64, 1)
    row = lax.broadcasted_iota(jnp.int32, (16, 256), 0)
    rest = jnp.where(row < 3, tap[9], jnp.where(row < 6, jnp.concatenate([x, x], axis=1), jnp.concatenate([biases[2:3]] * 2, axis=1)))
    high = rest.astype(BF16).astype(F32)
    mid = (rest - high).astype(BF16).astype(F32)
    low = rest - high - mid
    banded[BIAS : BIAS + 16, :] = jnp.where(row % 3 == 0, high, jnp.where(row % 3 == 1, mid, low)).astype(BF16)
    gap = lax.broadcasted_iota(jnp.int32, (32, 256), 0) - 2 * (lane_iota((32, 256)) // 32)
    for ky in range(3):
        for dx in range(2):
            band = jnp.zeros((32, 256), F32)
            for kx in range(3):
                band = jnp.where(gap == dx + kx, tap[3 * ky + kx], band)
            band = band.astype(BF16)
            for dy in range(2):
                phase = 2 * dy + dx
                at = 256 * phase + 64 * (ky + dy)
                banded[at : at + 32, :] = band

    for ky in range(3):
        for kx in range(3):
            at = 576 + 32 * (3 * ky + kx)
            w = packed[at : at + 32, 0:64]
            for dy in range(2):
                for dx in range(2):
                    r, c = ky + dy, kx + dx
                    lanes = slice(128 * dy + 64 * dx, 128 * dy + 64 * dx + 64)
                    at = T2 + 128 * r + 32 * c
                    banded[at : at + 32, lanes] = w
                    at = T2 + 512 + 128 * r + 32 * ((c + 2) % 4)
                    banded[at : at + 32, lanes] = w
            at = 64 * (3 * ky + kx)
            w = packed[at : at + 64, :]
            for dx in range(2):
                at = T3 + 256 * ky + 64 * (kx + dx)
                banded[at : at + 64, 128 * dx : 128 * dx + 128] = w


def plane_kernel(
    cfg, swap_a, raw, swap_b, banded, out,
    rs, dd, ff, ppe, ppo,
):
    zl, rows, width, dests, vb = cfg
    third_rows = rows // 8
    tiles = third_rows // 8 + 1
    period = tiles * 8
    m = zl * period
    groups = width // 16 + 1
    first = lax.axis_index("xy") == 0
    last = lax.axis_index("xy") == lax.axis_size("xy") - 1
    even = lax.axis_index("xy") % 2 == 0
    sub8 = lax.broadcasted_iota(jnp.int32, (1, 1, 8, 128), 2)
    keep = jnp.where(sub8 < 4, jnp.where(last, 0.0, 1.0), jnp.where(first, 0.0, 1.0))

    def masked(x):
        n, lanes = x.shape
        x = x.reshape(n // period, tiles, 8, lanes)
        k = jnp.concatenate([keep] * (lanes // 128), axis=3)
        return jnp.concatenate([x[:, :-1], x[:, -1:] * k], axis=1)

    for z in range(zl):
        a32, b32 = swap_a[z].astype(F32), swap_b[z].astype(F32)
        lo32, hi32 = jnp.where(even, b32, a32), jnp.where(even, a32, b32)
        raw32 = raw[z].astype(F32)
        end = 8 + 8 * period
        rs[z, 0] = jnp.zeros((end + 8, 128), F32)
        rs[z, width // 128 + 1] = jnp.zeros((end + 8, 128), F32)
        for t in range(width // 128):
            cols = slice(128 * t, 128 * t + 128)
            rs[z, t + 1, 0:8] = lo32[HALO - 8 :, cols]
            rs[z, t + 1, 8 : 8 + rows] = raw32[:, cols]
            rs[z, t + 1, 8 + rows : 8 + rows + HALO] = hi32[:, cols]
            rs[z, t + 1, 8 + rows + HALO : end - HALO] = jnp.zeros((8 * period - rows - 2 * HALO, 128), F32)
            rs[z, t + 1, end - HALO : end] = lo32[:, cols]
            rs[z, t + 1, end : end + 8] = raw32[0:8, cols]

    lane = lane_iota((period, 128))
    for g in range(groups):
        start = 16 * g + 125
        t, s = start // 128, start % 128
        left = 128 - s
        for z in range(zl):
            for k in range(5):
                def piece(phase, tile, amount):
                    x = rs[z, tile, pl.ds(8 + phase, period, stride=8), :]
                    return pltpu.roll(x, amount % 128, 1)

                a = piece(2 * k - 1, t, -s)
                b = piece(2 * k, t, 64 - s)
                if left < 18:
                    a = jnp.where(lane < left, a, piece(2 * k - 1, t + 1, -s))
                    b = jnp.where(lane < 64 + left, b, piece(2 * k, t + 1, 64 - s))
                dd[k, g * m + z * period : g * m + z * period + period, :] = jnp.where(lane < 64, a, b).astype(BF16)

    bias = [sum(banded[BIAS + 3 * i + j : BIAS + 3 * i + j + 1, :].astype(F32) for j in range(3)) for i in range(3)]
    bias1, bias2, bias3 = bias[0], bias[1][:, :128], bias[2][:, :128]

    chunk = 11 if groups % 11 == 0 else 1
    n = chunk * m
    for m1 in range(4):
        def level1(c, _, m1=m1):
            at = c * n
            x = jnp.concatenate([dd[m1, pl.ds(at, n), :], dd[m1 + 1, pl.ds(at, n), :]], axis=1)
            acc = None
            for phase in range(4):
                y = jnp.dot(x, banded[256 * phase : 256 * phase + 256, :], preferred_element_type=F32)
                acc = y if acc is None else jnp.maximum(acc, y)
            y = masked(jnp.maximum(acc + bias1, 0.0))
            row = m + c * n
            ff[m1 + 1, pl.ds(row, n), :] = y.reshape(n, 256).astype(BF16)
            if m1 == 0:
                ff[5, pl.ds(row, n), :] = shift_rows(y, False).reshape(n, 256).astype(BF16)
            if m1 == 3:
                ff[0, pl.ds(row, n), :] = shift_rows(y, True).reshape(n, 256).astype(BF16)
            return 0

        unrolled(groups // chunk, level1)
    for f in range(6):
        ff[f, 0:m, :] = jnp.zeros((m, 256), BF16)
        x = ff[f, m : 2 * m, 0:128].astype(F32)
        ff[f, m : 2 * m, 0:128] = jnp.where(lane_iota((m, 128)) < 32, 0.0, x).astype(BF16)
        x = ff[f, groups * m : (groups + 1) * m, 0:128].astype(F32)
        ff[f, groups * m : (groups + 1) * m, 0:128] = jnp.where(lane_iota((m, 128)) < 32, x, 0.0).astype(BF16)
        ff[f, groups * m : (groups + 1) * m, 128:256] = jnp.zeros((m, 128), BF16)

    def half(f, at, n, lanes):
        return ff[f, pl.ds(at, n), lanes : lanes + 128]

    def swapped(f, at_low, low, at_high, high, n):
        mask = lane_iota((n, 128)) < 64
        return jnp.where(mask, half(f, at_low, n, low), half(f, at_high, n, high))

    def level2(m2, at, n, even):
        low, high = [], []
        for r in range(4):
            f = 2 * m2 + r
            if even:
                low.append(swapped(f, at, 0, at - m, 128, n))
                high.append(half(f, at, n, 0))
            else:
                low.append(swapped(f, at, 128, at, 0, n))
                high.append(half(f, at, n, 128))
        low = jnp.dot(jnp.concatenate(low, axis=1), banded[T2 + 512 : T2 + 1024, :], preferred_element_type=F32)
        high = jnp.dot(jnp.concatenate(high, axis=1), banded[T2 : T2 + 512, :], preferred_element_type=F32)
        low = jnp.maximum(low[:, :128], low[:, 128:])
        high = jnp.maximum(high[:, :128], high[:, 128:])
        mask = lane_iota((n, 128)) < 64
        y = jnp.maximum(jnp.where(mask, low, high), pltpu.roll(jnp.where(mask, high, low), 64, 1))
        return masked(jnp.maximum(y + bias2, 0.0))

    for even, pp, count in ((True, ppe, groups), (False, ppo, groups - 1)):
        chunk = 11 if count % 11 == 0 else 8 if count % 8 == 0 else 1
        n = chunk * m
        for m2 in range(2):
            def step(c, _, m2=m2, even=even, pp=pp, n=n):
                at = c * n
                y = level2(m2, at + m, n, even)
                pp[m2 + 1, pl.ds(at, n), :] = y.reshape(n, 128).astype(BF16)
                if m2 == 0:
                    pp[3, pl.ds(at, n), :] = shift_rows(y, False).reshape(n, 128).astype(BF16)
                else:
                    pp[0, pl.ds(at, n), :] = shift_rows(y, True).reshape(n, 128).astype(BF16)
                return 0

            unrolled(count // chunk, step)
    for s in range(4):
        x = ppe[s, 0:m, :].astype(F32)
        ppe[s, 0:m, :] = jnp.where(lane_iota((m, 128)) < 64, 0.0, x).astype(BF16)
        at = (groups - 1) * m
        x = ppe[s, at : at + m, :].astype(F32)
        ppe[s, at : at + m, :] = jnp.where(lane_iota((m, 128)) < 64, x, 0.0).astype(BF16)

    def level3(at, n, odd):
        acc = None
        for dy in range(2):
            x = []
            for r in range(3):
                here = pl.ds(at, n)
                after = pl.ds(at + m, n)
                x += [ppo[dy + r, here, :], ppe[dy + r, after, :]] if odd else [ppe[dy + r, here, :], ppo[dy + r, here, :]]
            y = jnp.dot(jnp.concatenate(x, axis=1), banded[T3 : T3 + 768, :], preferred_element_type=F32)
            y = jnp.maximum(y[:, :128], y[:, 128:])
            acc = y if acc is None else jnp.maximum(acc, y)
        y = masked(jnp.maximum(acc + bias3, 0.0))
        return y.reshape(n // m, zl, tiles, 8, 128)

    zero = jnp.zeros((2 * (tiles - 1) + 1, zl * 8, 128), BF16)
    out[0, 0] = zero
    out[dests - 1, vb + 1] = zero
    chunk = 8
    n = chunk * m
    for c in range((groups - 1) // chunk):
        ys = [level3(c * n, n, odd) for odd in (False, True)]
        a, b = [y[:, :, tiles - 1].reshape(chunk * zl, 8, 128) for y in ys]
        sub = lax.broadcasted_iota(jnp.int32, a.shape, 1)
        edge = jnp.where(sub < 4, pltpu.roll(a, 2, 1), pltpu.roll(b, 6, 1))
        edge = edge.reshape(chunk, zl * 8, 128).astype(BF16)
        mains = [y[:, :, i].reshape(chunk, zl * 8, 128).astype(BF16) for y in ys for i in range(tiles - 1)]
        for w in range(chunk):
            v = c * chunk + w
            for d in range(dests):
                at = v - (vb * d - 1)
                if 0 <= at < vb + 2:
                    for i, part in enumerate(mains + [edge]):
                        out[d, at, i] = part[w]


def filter_kernel(send, wa, wb, ua, ub, sums, window):
    me = lax.axis_index("gz")
    pairs = window.shape[0]
    window[...] = send[me // 2, pl.ds((1 - me % 2) * (pairs - 2), pairs)]
    for i, (w, u) in enumerate(((wa, ua), (wb, ub))):
        chan = w.shape[3]
        total = jnp.zeros((1, w.shape[4]), F32)
        for kx in range(3):
            for dz in range(3):
                at = slice((3 * kx + dz) * chan, (3 * kx + dz + 1) * chan)
                g0, g1, g2 = (w[dz, ky, kx].astype(F32) for ky in range(3))
                outer, inner = 0.5 * (g0 + g2), 0.5 * g1
                u[0, at] = w[dz, 0, kx]
                u[1, at] = (outer + inner).astype(BF16)
                u[2, at] = (outer - inner).astype(BF16)
                u[3, at] = w[dz, 2, kx]
                total = total + jnp.sum(outer + inner, axis=0, keepdims=True)
        sums[i : i + 1] = total


def four_rows(x, level):
    x = x.reshape((x.shape[0] // 2, 2) + x.shape[1:])
    even, odd = x[:, 0], x[:, 1]
    return (even[:-1] - even[1:], odd[:-1] + even[1:] - level, even[1:] - odd[:-1], odd[:-1] - odd[1:])


def twice_mean(x):
    x = x.astype(F32).reshape(-1, 8, x.shape[-1])
    x = jnp.sum(jnp.sum(x, axis=0), axis=0, keepdims=True) * (2.0 / (x.shape[0] * 8 * x.shape[2]))
    return jnp.sum(x, axis=1, keepdims=True)


def cube_kernel(cfg, *refs):
    sources, zl, third_rows, vb, in_chan, mid_chan, out_chan, flip = cfg
    near, far = refs[: sources // 2], refs[sources // 2 : sources]
    ua, ba, ub, bb, sums, out, va, mid, vm, ms = refs[sources:]
    me = lax.axis_index("gz")
    depth = sources * zl
    xs = 2 * vb
    tiles = third_rows // 8

    rows = 8 * depth
    shape = (rows, rows)
    to = lax.broadcasted_iota(jnp.int32, shape, 0)
    at = lax.broadcasted_iota(jnp.int32, shape, 1)
    k_to, z_to = to // depth, to % depth
    k_at, z_at = at % 8, ((at // (8 * zl)) ^ me) * zl + (at // 8) % zl
    gather = jnp.concatenate(
        [jnp.where((k_to == k_at) & (z_at == z_to + dz), 1.0, 0.0).astype(BF16) for dz in (-1, 0, 1)], axis=0
    )
    parts = 2 * tiles + 1
    level_a = twice_mean(near[0][...])
    for vl in range(vb + 2):
        y = []
        for c in range(parts):
            x = jnp.concatenate(
                [part for k in range(sources // 2) for part in (near[k][(me % 2) * vb + vl, c], far[k][vl, c])], axis=0
            )
            y.append(jnp.dot(gather, x, preferred_element_type=F32).reshape(3, 8, depth, in_chan))
        for side in range(2):
            for dz in range(3):
                edge = y[parts - 1][dz, 4 * side : 4 * side + 4]
                x = [edge[0:2]] + [y[side * tiles + i][dz] for i in range(tiles)] + [edge[2:4]]
                for t, v in enumerate(four_rows(jnp.concatenate(x, axis=0), level_a)):
                    va[t, :, 2 * vl + side, :, dz * in_chan : (dz + 1) * in_chan] = v.astype(BF16)

    mid_x = xs + 2
    mid_rows = third_rows + 2
    pairs_a = mid_rows // 2

    def products(v, u, first, count, breadth, chan):
        n = count * breadth * depth
        slot = (first // count) % 2
        for t in range(4):
            x = jnp.concatenate([v[t, first : first + count, kx : kx + breadth].reshape(n, 3 * chan) for kx in range(3)], axis=1)
            ms[slot, t, 0:n] = jnp.dot(x, u[t], preferred_element_type=F32)
        m1, m2 = ms[slot, 1, 0:n], ms[slot, 2, 0:n]
        return ms[slot, 0, 0:n] + (m1 + m2), (m1 - m2) - ms[slot, 3, 0:n]

    step = 3 if pairs_a % 3 == 0 else 1
    bias = ba[...] + level_a * sums[0:1]
    for first in range(0, pairs_a, step):
        ys = [jnp.maximum(y + bias, 0.0).astype(BF16) for y in products(va, ua, first, step, mid_x, in_chan)]
        for i, y in enumerate(ys):
            y = y.reshape(step, mid_x, depth, mid_chan)
            for j in range(step):
                mid[2 * (first + j) + i] = y[j]

    row, col = lax.axis_index("xy"), lax.axis_index("gz")

    @pl.when(row == 0)
    def _():
        mid[0] = jnp.zeros(mid.shape[1:], BF16)

    @pl.when(row == lax.axis_size("xy") - 1)
    def _():
        mid[mid_rows - 1] = jnp.zeros(mid.shape[1:], BF16)

    @pl.when(col == 0)
    def _():
        mid[:, 0] = jnp.zeros(mid.shape[:1] + mid.shape[2:], BF16)

    @pl.when(col == lax.axis_size("gz") - 1)
    def _():
        mid[:, mid_x - 1] = jnp.zeros(mid.shape[:1] + mid.shape[2:], BF16)

    pairs_b = third_rows // 2
    level_b = twice_mean(mid[4:8])
    bias = bb[...] + level_b * sums[1:2]
    step = 4 if pairs_b % 4 == 0 else 1
    if flip:
        n = xs * depth
        to = lax.broadcasted_iota(jnp.int32, (n, n), 0)
        at = lax.broadcasted_iota(jnp.int32, (n, n), 1)
        turn = jnp.where((to // xs == at % depth) & (to % xs == at // depth), 1.0, 0.0).astype(BF16)
    for first in range(0, pairs_b, step):
        for x_at in range(mid_x):
            x = mid[2 * first : 2 * (first + step) + 2, x_at].astype(F32)
            for t, v in enumerate(four_rows(x, level_b)):
                here = v.shape
                vm[t, first : first + step, x_at, :, mid_chan : 2 * mid_chan] = v.astype(BF16)
                v = v.reshape(step, depth // 8, 8, mid_chan)
                sub = lax.broadcasted_iota(jnp.int32, v.shape, 2)
                none = jnp.zeros_like(v[:, :1])
                if t == 1:
                    none = none - level_b
                rolled = pltpu.roll(v, 1, 2)
                moved = jnp.where(sub == 0, jnp.concatenate([none, rolled[:, :-1]], axis=1), rolled)
                vm[t, first : first + step, x_at, :, 0:mid_chan] = moved.reshape(here).astype(BF16)
                rolled = pltpu.roll(v, 7, 2)
                moved = jnp.where(sub == 7, jnp.concatenate([rolled[:, 1:], none], axis=1), rolled)
                vm[t, first : first + step, x_at, :, 2 * mid_chan :] = moved.reshape(here).astype(BF16)
        for i, y in enumerate(products(vm, ub, first, step, xs, mid_chan)):
            y = jnp.maximum(y + bias, 0.0).astype(BF16)
            if flip:
                y = y.reshape(step, xs * depth, out_chan)
                for j in range(step):
                    t = jnp.dot(turn, y[j], preferred_element_type=F32).astype(BF16)
                    out[:, 2 * (first + j) + i] = t.reshape(depth, xs, out_chan)
            else:
                y = y.reshape(step, xs, depth, out_chan)
                for j in range(step):
                    out[2 * (first + j) + i] = y[j]


def body(
    raw_volume,
    weight_first,
    bias_first,
    weight_second,
    bias_second,
    weight_third,
    bias_third,
    weight_iso_a,
    bias_iso_a,
    weight_iso_b,
    bias_iso_b,
):
    zl, rows, width = raw_volume.shape
    dests = lax.axis_size("gz")
    depth = zl * dests
    third_rows = rows // 8
    vb = width // 8 // dests // 2
    count = lax.axis_size("xy")
    even = lax.axis_index("xy") % 2 == 0

    def swap(start, pairs):
        edge = lax.dynamic_slice_in_dim(raw_volume, start, HALO, axis=1)
        return lax.ppermute(edge, "xy", [(i, i + 1) for i in pairs] + [(i + 1, i) for i in pairs])

    first = swap(jnp.where(even, rows - HALO, 0), range(0, count - 1, 2))
    second = swap(jnp.where(even, 0, rows - HALO), range(1, count - 1, 2))

    period = third_rows + 8
    m = zl * period
    groups = width // 16 + 1
    parts = 2 * (third_rows // 8) + 1
    def wide(x, count):
        return jnp.pad(x, ((0, count - x.shape[0]), (0, 128 - x.shape[1])))

    packed = jnp.concatenate(
        [
            jnp.transpose(weight_third, (2, 3, 1, 0)).reshape(576, 128),
            wide(jnp.transpose(weight_second, (2, 3, 1, 0)).reshape(288, 64), 288),
            wide(jnp.transpose(weight_first, (1, 2, 3, 0)).reshape(9, 32), 16),
        ],
        axis=0,
    )
    biases = jnp.concatenate([wide(x[None], 1) for x in (bias_first, bias_second, bias_third)] + [jnp.zeros((5, 128), F32)])
    banded = pl.pallas_call(
        weight_kernel,
        out_shape=jax.ShapeDtypeStruct((BIAS + 16, 256), BF16),
        in_specs=[VMEM] * 2,
        out_specs=VMEM,
        scratch_shapes=[pltpu.VMEM((16, 128), F32)],
        compiler_params=pltpu.CompilerParams(vmem_limit_bytes=20 << 20),
        cost_estimate=pl.CostEstimate(flops=2000000000, bytes_accessed=2000000, transcendentals=0),
        name="weights",
    )(packed, biases)
    chips = dests // 2
    send = pl.pallas_call(
        functools.partial(plane_kernel, (zl, rows, width, chips, 2 * vb)),
        out_shape=jax.ShapeDtypeStruct((chips, 2 * vb + 2, parts, zl * 8, 128), BF16),
        in_specs=[VMEM] * 4,
        out_specs=VMEM,
        scratch_shapes=[
            pltpu.VMEM((zl, width // 128 + 2, 8 * period + 16, 128), F32),
            pltpu.VMEM((5, groups * m, 128), BF16),
            pltpu.VMEM((6, (groups + 1) * m, 256), BF16),
            pltpu.VMEM((4, groups * m, 128), BF16),
            pltpu.VMEM((4, (groups - 1) * m, 128), BF16),
        ],
        compiler_params=pltpu.CompilerParams(vmem_limit_bytes=20 << 20),
        name="planes",
    )(first, raw_volume, second, banded)
    me = lax.axis_index("gz")
    other = (1 - me % 2) * vb
    kernels = (weight_iso_a, weight_iso_b)
    ua, ub, sums, own = pl.pallas_call(
        filter_kernel,
        out_shape=[jax.ShapeDtypeStruct((4, 9 * w.shape[3], w.shape[4]), BF16) for w in kernels]
        + [
            jax.ShapeDtypeStruct((2, weight_iso_b.shape[4]), F32),
            jax.ShapeDtypeStruct((vb + 2,) + send.shape[2:], BF16),
        ],
        in_specs=[VMEM] * 3,
        out_specs=[VMEM] * 4,
        compiler_params=pltpu.CompilerParams(vmem_limit_bytes=20 << 20),
        cost_estimate=pl.CostEstimate(flops=4000000000, bytes_accessed=8000000, transcendentals=0),
        name="filters",
    )(send, *kernels)
    near, far = [], []
    for k in range(chips):
        block = lax.dynamic_index_in_dim(send, (me // 2) ^ k, 0, keepdims=False)
        if k:
            block = lax.ppermute(block, "gz", [(i, i ^ (2 * k)) for i in range(dests)])
        near.append(block)
        window = lax.dynamic_slice_in_dim(block, other, vb + 2, axis=0) if k else own
        far.append(lax.ppermute(window, "gz", [(i, i ^ 1) for i in range(dests)]))

    xs = 2 * vb
    in_chan, mid_chan = weight_iso_a.shape[3:]
    out_chan = weight_iso_b.shape[4]
    flip = xs % 8 == 0
    shape = (depth, third_rows, xs, out_chan) if flip else (third_rows, xs, depth, out_chan)
    out = pl.pallas_call(
        functools.partial(cube_kernel, (dests, zl, third_rows, vb, in_chan, mid_chan, out_chan, flip)),
        out_shape=jax.ShapeDtypeStruct(shape, BF16),
        in_specs=[VMEM] * (dests + 5),
        out_specs=VMEM,
        scratch_shapes=[
            pltpu.VMEM((4, third_rows // 2 + 1, xs + 4, depth, 3 * in_chan), BF16),
            pltpu.VMEM((third_rows + 2, xs + 2, depth, mid_chan), BF16),
            pltpu.VMEM((4, third_rows // 2, xs + 2, depth, 3 * mid_chan), BF16),
            pltpu.VMEM((2, 4, max(3 * (xs + 2), 4 * xs) * depth, mid_chan), F32),
        ],
        compiler_params=pltpu.CompilerParams(vmem_limit_bytes=(36 if depth <= 16 else 60) << 20),
        name="cubes",
    )(*near, *far, ua, bias_iso_a[None], ub, bias_iso_b[None], sums)
    return out if flip else jnp.transpose(out, (2, 0, 1, 3))


def solution(mesh):
    placed = (P("gz", "xy", None), P(), P(), P(), P(), P(), P(), P(), P(), P(), P())
    return jax.shard_map(
        body, mesh=mesh, in_specs=placed, out_specs=P(None, "xy", "gz", None), check_vma=False
    )
```

```python
import functools

import jax
import jax.numpy as jnp
from jax import lax
from jax.experimental import pallas as pl
from jax.experimental.pallas import tpu as pltpu
from jax.sharding import PartitionSpec as P

T2, T3, BIAS = 1024, 2048, 2816
HALO = 24
VMEM = pl.BlockSpec(memory_space=pltpu.VMEM)
F32 = jnp.float32
BF16 = jnp.bfloat16


def unrolled(count, step):
    for i in range(count):
        step(i, 0)


def lane_iota(shape):
    return lax.broadcasted_iota(jnp.int32, shape, len(shape) - 1)


def shift_rows(x, down):
    sub = lax.broadcasted_iota(jnp.int32, x.shape, 2)
    if down:
        rolled = pltpu.roll(x, 1, 2)
        other = jnp.concatenate([rolled[:, -1:], rolled[:, :-1]], axis=1)
        return jnp.where(sub == 0, other, rolled)
    rolled = pltpu.roll(x, 7, 2)
    other = jnp.concatenate([rolled[:, 1:], rolled[:, :1]], axis=1)
    return jnp.where(sub == 7, other, rolled)


def tile_lanes(ref, row):
    x = ref[row : row + 1, :]
    return x + pltpu.roll(x, 32, 1) + pltpu.roll(x, 64, 1) + pltpu.roll(x, 96, 1)


def weight_kernel(packed, biases, raw, banded, small):
    small[0:16] = packed[864:880].astype(F32)
    small[9:11] = biases[0:2]
    tap = []
    for i in range(10):
        x = tile_lanes(small, i)
        tap.append(jnp.concatenate([x, x], axis=1))
    banded[...] = jnp.zeros_like(banded)
    x = small[10:11, :]
    x = x + pltpu.roll(x, 64, 1)
    row = lax.broadcasted_iota(jnp.int32, (16, 256), 0)
    rest = jnp.where(row < 3, tap[9], jnp.where(row < 6, jnp.concatenate([x, x], axis=1), jnp.concatenate([biases[2:3]] * 2, axis=1)))
    high = rest.astype(BF16).astype(F32)
    mid = (rest - high).astype(BF16).astype(F32)
    low = rest - high - mid
    banded[BIAS : BIAS + 16, :] = jnp.where(row % 3 == 0, high, jnp.where(row % 3 == 1, mid, low)).astype(BF16)
    gap = lax.broadcasted_iota(jnp.int32, (32, 256), 0) - 2 * (lane_iota((32, 256)) // 32)
    for ky in range(3):
        for dx in range(2):
            band = jnp.zeros((32, 256), F32)
            for kx in range(3):
                band = jnp.where(gap == dx + kx, tap[3 * ky + kx], band)
            band = band.astype(BF16)
            for dy in range(2):
                phase = 2 * dy + dx
                at = 256 * phase + 64 * (ky + dy)
                banded[at : at + 32, :] = band

    for ky in range(3):
        for kx in range(3):
            at = 576 + 32 * (3 * ky + kx)
            w = packed[at : at + 32, 0:64]
            for dy in range(2):
                for dx in range(2):
                    r, c = ky + dy, kx + dx
                    lanes = slice(128 * dy + 64 * dx, 128 * dy + 64 * dx + 64)
                    at = T2 + 128 * r + 32 * c
                    banded[at : at + 32, lanes] = w
                    at = T2 + 512 + 128 * r + 32 * ((c + 2) % 4)
                    banded[at : at + 32, lanes] = w
            at = 64 * (3 * ky + kx)
            w = packed[at : at + 64, :]
            for dx in range(2):
                at = T3 + 256 * ky + 64 * (kx + dx)
                banded[at : at + 64, 128 * dx : 128 * dx + 128] = w


def plane_kernel(
    cfg, swap_a, raw, swap_b, banded, out,
    rs, dd, ff, ppe, ppo,
):
    zl, rows, width, dests, vb = cfg
    third_rows = rows // 8
    tiles = third_rows // 8 + 1
    period = tiles * 8
    m = zl * period
    groups = width // 16 + 1
    first = lax.axis_index("xy") == 0
    last = lax.axis_index("xy") == lax.axis_size("xy") - 1
    even = lax.axis_index("xy") % 2 == 0
    sub8 = lax.broadcasted_iota(jnp.int32, (1, 1, 8, 128), 2)
    keep = jnp.where(sub8 < 4, jnp.where(last, 0.0, 1.0), jnp.where(first, 0.0, 1.0))

    def masked(x):
        n, lanes = x.shape
        x = x.reshape(n // period, tiles, 8, lanes)
        k = jnp.concatenate([keep] * (lanes // 128), axis=3)
        return jnp.concatenate([x[:, :-1], x[:, -1:] * k], axis=1)

    for z in range(zl):
        a32, b32 = swap_a[z].astype(F32), swap_b[z].astype(F32)
        lo32, hi32 = jnp.where(even, b32, a32), jnp.where(even, a32, b32)
        raw32 = raw[z].astype(F32)
        end = 8 + 8 * period
        rs[z, 0] = jnp.zeros((end + 8, 128), F32)
        rs[z, width // 128 + 1] = jnp.zeros((end + 8, 128), F32)
        for t in range(width // 128):
            cols = slice(128 * t, 128 * t + 128)
            rs[z, t + 1, 0:8] = lo32[HALO - 8 :, cols]
            rs[z, t + 1, 8 : 8 + rows] = raw32[:, cols]
            rs[z, t + 1, 8 + rows : 8 + rows + HALO] = hi32[:, cols]
            rs[z, t + 1, 8 + rows + HALO : end - HALO] = jnp.zeros((8 * period - rows - 2 * HALO, 128), F32)
            rs[z, t + 1, end - HALO : end] = lo32[:, cols]
            rs[z, t + 1, end : end + 8] = raw32[0:8, cols]

    lane = lane_iota((period, 128))
    for g in range(groups):
        start = 16 * g + 125
        t, s = start // 128, start % 128
        left = 128 - s
        for z in range(zl):
            for k in range(5):
                def piece(phase, tile, amount):
                    x = rs[z, tile, pl.ds(8 + phase, period, stride=8), :]
                    return pltpu.roll(x, amount % 128, 1)

                a = piece(2 * k - 1, t, -s)
                b = piece(2 * k, t, 64 - s)
                if left < 18:
                    a = jnp.where(lane < left, a, piece(2 * k - 1, t + 1, -s))
                    b = jnp.where(lane < 64 + left, b, piece(2 * k, t + 1, 64 - s))
                dd[k, g * m + z * period : g * m + z * period + period, :] = jnp.where(lane < 64, a, b).astype(BF16)

    bias = [sum(banded[BIAS + 3 * i + j : BIAS + 3 * i + j + 1, :].astype(F32) for j in range(3)) for i in range(3)]
    bias1, bias2, bias3 = bias[0], bias[1][:, :128], bias[2][:, :128]

    chunk = 11 if groups % 11 == 0 else 1
    n = chunk * m
    for m1 in range(4):
        def level1(c, _, m1=m1):
            at = c * n
            x = jnp.concatenate([dd[m1, pl.ds(at, n), :], dd[m1 + 1, pl.ds(at, n), :]], axis=1)
            acc = None
            for phase in range(4):
                y = jnp.dot(x, banded[256 * phase : 256 * phase + 256, :], preferred_element_type=F32)
                acc = y if acc is None else jnp.maximum(acc, y)
            y = masked(jnp.maximum(acc + bias1, 0.0))
            row = m + c * n
            ff[m1 + 1, pl.ds(row, n), :] = y.reshape(n, 256).astype(BF16)
            if m1 == 0:
                ff[5, pl.ds(row, n), :] = shift_rows(y, False).reshape(n, 256).astype(BF16)
            if m1 == 3:
                ff[0, pl.ds(row, n), :] = shift_rows(y, True).reshape(n, 256).astype(BF16)
            return 0

        unrolled(groups // chunk, level1)
    for f in range(6):
        ff[f, 0:m, :] = jnp.zeros((m, 256), BF16)
        x = ff[f, m : 2 * m, 0:128].astype(F32)
        ff[f, m : 2 * m, 0:128] = jnp.where(lane_iota((m, 128)) < 32, 0.0, x).astype(BF16)
        x = ff[f, groups * m : (groups + 1) * m, 0:128].astype(F32)
        ff[f, groups * m : (groups + 1) * m, 0:128] = jnp.where(lane_iota((m, 128)) < 32, x, 0.0).astype(BF16)
        ff[f, groups * m : (groups + 1) * m, 128:256] = jnp.zeros((m, 128), BF16)

    def half(f, at, n, lanes):
        return ff[f, pl.ds(at, n), lanes : lanes + 128]

    def swapped(f, at_low, low, at_high, high, n):
        mask = lane_iota((n, 128)) < 64
        return jnp.where(mask, half(f, at_low, n, low), half(f, at_high, n, high))

    def level2(m2, at, n, even):
        low, high = [], []
        for r in range(4):
            f = 2 * m2 + r
            if even:
                low.append(swapped(f, at, 0, at - m, 128, n))
                high.append(half(f, at, n, 0))
            else:
                low.append(swapped(f, at, 128, at, 0, n))
                high.append(half(f, at, n, 128))
        low = jnp.dot(jnp.concatenate(low, axis=1), banded[T2 + 512 : T2 + 1024, :], preferred_element_type=F32)
        high = jnp.dot(jnp.concatenate(high, axis=1), banded[T2 : T2 + 512, :], preferred_element_type=F32)
        low = jnp.maximum(low[:, :128], low[:, 128:])
        high = jnp.maximum(high[:, :128], high[:, 128:])
        mask = lane_iota((n, 128)) < 64
        y = jnp.maximum(jnp.where(mask, low, high), pltpu.roll(jnp.where(mask, high, low), 64, 1))
        return masked(jnp.maximum(y + bias2, 0.0))

    for even, pp, count in ((True, ppe, groups), (False, ppo, groups - 1)):
        chunk = 11 if count % 11 == 0 else 8 if count % 8 == 0 else 1
        n = chunk * m
        for m2 in range(2):
            def step(c, _, m2=m2, even=even, pp=pp, n=n):
                at = c * n
                y = level2(m2, at + m, n, even)
                pp[m2 + 1, pl.ds(at, n), :] = y.reshape(n, 128).astype(BF16)
                if m2 == 0:
                    pp[3, pl.ds(at, n), :] = shift_rows(y, False).reshape(n, 128).astype(BF16)
                else:
                    pp[0, pl.ds(at, n), :] = shift_rows(y, True).reshape(n, 128).astype(BF16)
                return 0

            unrolled(count // chunk, step)
    for s in range(4):
        x = ppe[s, 0:m, :].astype(F32)
        ppe[s, 0:m, :] = jnp.where(lane_iota((m, 128)) < 64, 0.0, x).astype(BF16)
        at = (groups - 1) * m
        x = ppe[s, at : at + m, :].astype(F32)
        ppe[s, at : at + m, :] = jnp.where(lane_iota((m, 128)) < 64, x, 0.0).astype(BF16)

    def level3(at, n, odd):
        acc = None
        for dy in range(2):
            x = []
            for r in range(3):
                here = pl.ds(at, n)
                after = pl.ds(at + m, n)
                x += [ppo[dy + r, here, :], ppe[dy + r, after, :]] if odd else [ppe[dy + r, here, :], ppo[dy + r, here, :]]
            y = jnp.dot(jnp.concatenate(x, axis=1), banded[T3 : T3 + 768, :], preferred_element_type=F32)
            y = jnp.maximum(y[:, :128], y[:, 128:])
            acc = y if acc is None else jnp.maximum(acc, y)
        y = masked(jnp.maximum(acc + bias3, 0.0))
        return y.reshape(n // m, zl, tiles, 8, 128)

    zero = jnp.zeros((2 * (tiles - 1) + 1, zl * 8, 128), BF16)
    out[0, 0] = zero
    out[dests - 1, vb + 1] = zero
    chunk = 8
    n = chunk * m
    for c in range((groups - 1) // chunk):
        ys = [level3(c * n, n, odd) for odd in (False, True)]
        a, b = [y[:, :, tiles - 1].reshape(chunk * zl, 8, 128) for y in ys]
        sub = lax.broadcasted_iota(jnp.int32, a.shape, 1)
        edge = jnp.where(sub < 4, pltpu.roll(a, 2, 1), pltpu.roll(b, 6, 1))
        edge = edge.reshape(chunk, zl * 8, 128).astype(BF16)
        mains = [y[:, :, i].reshape(chunk, zl * 8, 128).astype(BF16) for y in ys for i in range(tiles - 1)]
        for w in range(chunk):
            v = c * chunk + w
            for d in range(dests):
                at = v - (vb * d - 1)
                if 0 <= at < vb + 2:
                    for i, part in enumerate(mains + [edge]):
                        out[d, at, i] = part[w]


def filter_kernel(send, wa, wb, ua, ub, sums, window):
    me = lax.axis_index("gz")
    pairs = window.shape[0]
    window[...] = send[me // 2, pl.ds((1 - me % 2) * (pairs - 2), pairs)]
    for i, (w, u) in enumerate(((wa, ua), (wb, ub))):
        chan = w.shape[3]
        total = jnp.zeros((1, w.shape[4]), F32)
        for kx in range(3):
            for dz in range(3):
                at = slice((3 * kx + dz) * chan, (3 * kx + dz + 1) * chan)
                g0, g1, g2 = (w[dz, ky, kx].astype(F32) for ky in range(3))
                outer, inner = 0.5 * (g0 + g2), 0.5 * g1
                u[0, at] = w[dz, 0, kx]
                u[1, at] = (outer + inner).astype(BF16)
                u[2, at] = (outer - inner).astype(BF16)
                u[3, at] = w[dz, 2, kx]
                total = total + jnp.sum(outer + inner, axis=0, keepdims=True)
        sums[i : i + 1] = total


def four_rows(x, level):
    x = x.reshape((x.shape[0] // 2, 2) + x.shape[1:])
    even, odd = x[:, 0], x[:, 1]
    return (even[:-1] - even[1:], odd[:-1] + even[1:] - level, even[1:] - odd[:-1], odd[:-1] - odd[1:])


def twice_mean(x):
    x = x.astype(F32).reshape(-1, 8, x.shape[-1])
    x = jnp.sum(jnp.sum(x, axis=0), axis=0, keepdims=True) * (2.0 / (x.shape[0] * 8 * x.shape[2]))
    return jnp.sum(x, axis=1, keepdims=True)


def cube_kernel(cfg, *refs):
    sources, zl, third_rows, vb, in_chan, mid_chan, out_chan, flip = cfg
    near, far = refs[: sources // 2], refs[sources // 2 : sources]
    ua, ba, ub, bb, sums, out, va, mid, vm, ms = refs[sources:]
    me = lax.axis_index("gz")
    depth = sources * zl
    xs = 2 * vb
    tiles = third_rows // 8

    rows = 8 * depth
    shape = (rows, rows)
    to = lax.broadcasted_iota(jnp.int32, shape, 0)
    at = lax.broadcasted_iota(jnp.int32, shape, 1)
    k_to, z_to = to // depth, to % depth
    k_at, z_at = at % 8, ((at // (8 * zl)) ^ me) * zl + (at // 8) % zl
    gather = jnp.concatenate(
        [jnp.where((k_to == k_at) & (z_at == z_to + dz), 1.0, 0.0).astype(BF16) for dz in (-1, 0, 1)], axis=0
    )
    parts = 2 * tiles + 1
    level_a = twice_mean(near[0][...])
    for vl in range(vb + 2):
        y = []
        for c in range(parts):
            x = jnp.concatenate(
                [part for k in range(sources // 2) for part in (near[k][(me % 2) * vb + vl, c], far[k][vl, c])], axis=0
            )
            y.append(jnp.dot(gather, x, preferred_element_type=F32).reshape(3, 8, depth, in_chan))
        for side in range(2):
            for dz in range(3):
                edge = y[parts - 1][dz, 4 * side : 4 * side + 4]
                x = [edge[0:2]] + [y[side * tiles + i][dz] for i in range(tiles)] + [edge[2:4]]
                for t, v in enumerate(four_rows(jnp.concatenate(x, axis=0), level_a)):
                    va[t, :, 2 * vl + side, :, dz * in_chan : (dz + 1) * in_chan] = v.astype(BF16)

    mid_x = xs + 2
    mid_rows = third_rows + 2
    pairs_a = mid_rows // 2

    def products(v, u, first, count, breadth, chan):
        n = count * breadth * depth
        slot = (first // count) % 2
        for t in range(4):
            x = jnp.concatenate([v[t, first : first + count, kx : kx + breadth].reshape(n, 3 * chan) for kx in range(3)], axis=1)
            ms[slot, t, 0:n] = jnp.dot(x, u[t], preferred_element_type=F32)
        m1, m2 = ms[slot, 1, 0:n], ms[slot, 2, 0:n]
        return ms[slot, 0, 0:n] + (m1 + m2), (m1 - m2) - ms[slot, 3, 0:n]

    step = 3 if pairs_a % 3 == 0 else 1
    bias = ba[...] + level_a * sums[0:1]
    for first in range(0, pairs_a, step):
        ys = [jnp.maximum(y + bias, 0.0).astype(BF16) for y in products(va, ua, first, step, mid_x, in_chan)]
        for i, y in enumerate(ys):
            y = y.reshape(step, mid_x, depth, mid_chan)
            for j in range(step):
                mid[2 * (first + j) + i] = y[j]

    row, col = lax.axis_index("xy"), lax.axis_index("gz")

    @pl.when(row == 0)
    def _():
        mid[0] = jnp.zeros(mid.shape[1:], BF16)

    @pl.when(row == lax.axis_size("xy") - 1)
    def _():
        mid[mid_rows - 1] = jnp.zeros(mid.shape[1:], BF16)

    @pl.when(col == 0)
    def _():
        mid[:, 0] = jnp.zeros(mid.shape[:1] + mid.shape[2:], BF16)

    @pl.when(col == lax.axis_size("gz") - 1)
    def _():
        mid[:, mid_x - 1] = jnp.zeros(mid.shape[:1] + mid.shape[2:], BF16)

    pairs_b = third_rows // 2
    level_b = twice_mean(mid[4:8])
    bias = bb[...] + level_b * sums[1:2]
    step = 4 if pairs_b % 4 == 0 else 1
    if flip:
        n = xs * depth
        to = lax.broadcasted_iota(jnp.int32, (n, n), 0)
        at = lax.broadcasted_iota(jnp.int32, (n, n), 1)
        turn = jnp.where((to // xs == at % depth) & (to % xs == at // depth), 1.0, 0.0).astype(BF16)
    for first in range(0, pairs_b, step):
        for x_at in range(mid_x):
            x = mid[2 * first : 2 * (first + step) + 2, x_at].astype(F32)
            for t, v in enumerate(four_rows(x, level_b)):
                here = v.shape
                vm[t, first : first + step, x_at, :, mid_chan : 2 * mid_chan] = v.astype(BF16)
                v = v.reshape(step, depth // 8, 8, mid_chan)
                sub = lax.broadcasted_iota(jnp.int32, v.shape, 2)
                none = jnp.zeros_like(v[:, :1])
                if t == 1:
                    none = none - level_b
                rolled = pltpu.roll(v, 1, 2)
                moved = jnp.where(sub == 0, jnp.concatenate([none, rolled[:, :-1]], axis=1), rolled)
                vm[t, first : first + step, x_at, :, 0:mid_chan] = moved.reshape(here).astype(BF16)
                rolled = pltpu.roll(v, 7, 2)
                moved = jnp.where(sub == 7, jnp.concatenate([rolled[:, 1:], none], axis=1), rolled)
                vm[t, first : first + step, x_at, :, 2 * mid_chan :] = moved.reshape(here).astype(BF16)
        for i, y in enumerate(products(vm, ub, first, step, xs, mid_chan)):
            y = jnp.maximum(y + bias, 0.0).astype(BF16)
            if flip:
                y = y.reshape(step, xs * depth, out_chan)
                for j in range(step):
                    t = jnp.dot(turn, y[j], preferred_element_type=F32).astype(BF16)
                    out[:, 2 * (first + j) + i] = t.reshape(depth, xs, out_chan)
            else:
                y = y.reshape(step, xs, depth, out_chan)
                for j in range(step):
                    out[2 * (first + j) + i] = y[j]


def body(
    raw_volume,
    weight_first,
    bias_first,
    weight_second,
    bias_second,
    weight_third,
    bias_third,
    weight_iso_a,
    bias_iso_a,
    weight_iso_b,
    bias_iso_b,
):
    zl, rows, width = raw_volume.shape
    dests = lax.axis_size("gz")
    depth = zl * dests
    third_rows = rows // 8
    vb = width // 8 // dests // 2
    count = lax.axis_size("xy")
    even = lax.axis_index("xy") % 2 == 0

    def swap(start, pairs):
        edge = lax.dynamic_slice_in_dim(raw_volume, start, HALO, axis=1)
        return lax.ppermute(edge, "xy", [(i, i + 1) for i in pairs] + [(i + 1, i) for i in pairs])

    first = swap(jnp.where(even, rows - HALO, 0), range(0, count - 1, 2))
    second = swap(jnp.where(even, 0, rows - HALO), range(1, count - 1, 2))

    period = third_rows + 8
    m = zl * period
    groups = width // 16 + 1
    parts = 2 * (third_rows // 8) + 1
    def wide(x, count):
        return jnp.pad(x, ((0, count - x.shape[0]), (0, 128 - x.shape[1])))

    packed = jnp.concatenate(
        [
            jnp.transpose(weight_third, (2, 3, 1, 0)).reshape(576, 128),
            wide(jnp.transpose(weight_second, (2, 3, 1, 0)).reshape(288, 64), 288),
            wide(jnp.transpose(weight_first, (1, 2, 3, 0)).reshape(9, 32), 16),
        ],
        axis=0,
    )
    biases = jnp.concatenate([wide(x[None], 1) for x in (bias_first, bias_second, bias_third)] + [jnp.zeros((5, 128), F32)])
    banded = pl.pallas_call(
        weight_kernel,
        out_shape=jax.ShapeDtypeStruct((BIAS + 16, 256), BF16),
        in_specs=[VMEM] * 3,
        out_specs=VMEM,
        scratch_shapes=[pltpu.VMEM((16, 128), F32)],
        compiler_params=pltpu.CompilerParams(vmem_limit_bytes=20 << 20),
        cost_estimate=pl.CostEstimate(flops=2000000000, bytes_accessed=2000000, transcendentals=0),
        name="weights",
    )(packed, biases, raw_volume)
    chips = dests // 2
    send = pl.pallas_call(
        functools.partial(plane_kernel, (zl, rows, width, chips, 2 * vb)),
        out_shape=jax.ShapeDtypeStruct((chips, 2 * vb + 2, parts, zl * 8, 128), BF16),
        in_specs=[VMEM] * 4,
        out_specs=VMEM,
        scratch_shapes=[
            pltpu.VMEM((zl, width // 128 + 2, 8 * period + 16, 128), F32),
            pltpu.VMEM((5, groups * m, 128), BF16),
            pltpu.VMEM((6, (groups + 1) * m, 256), BF16),
            pltpu.VMEM((4, groups * m, 128), BF16),
            pltpu.VMEM((4, (groups - 1) * m, 128), BF16),
        ],
        compiler_params=pltpu.CompilerParams(vmem_limit_bytes=20 << 20),
        name="planes",
    )(first, raw_volume, second, banded)
    me = lax.axis_index("gz")
    other = (1 - me % 2) * vb
    kernels = (weight_iso_a, weight_iso_b)
    ua, ub, sums, own = pl.pallas_call(
        filter_kernel,
        out_shape=[jax.ShapeDtypeStruct((4, 9 * w.shape[3], w.shape[4]), BF16) for w in kernels]
        + [
            jax.ShapeDtypeStruct((2, weight_iso_b.shape[4]), F32),
            jax.ShapeDtypeStruct((vb + 2,) + send.shape[2:], BF16),
        ],
        in_specs=[VMEM] * 3,
        out_specs=[VMEM] * 4,
        compiler_params=pltpu.CompilerParams(vmem_limit_bytes=20 << 20),
        cost_estimate=pl.CostEstimate(flops=4000000000, bytes_accessed=8000000, transcendentals=0),
        name="filters",
    )(send, *kernels)
    near, far = [], []
    for k in range(chips):
        block = lax.dynamic_index_in_dim(send, (me // 2) ^ k, 0, keepdims=False)
        if k:
            block = lax.ppermute(block, "gz", [(i, i ^ (2 * k)) for i in range(dests)])
        near.append(block)
        window = lax.dynamic_slice_in_dim(block, other, vb + 2, axis=0) if k else own
        far.append(lax.ppermute(window, "gz", [(i, i ^ 1) for i in range(dests)]))

    xs = 2 * vb
    in_chan, mid_chan = weight_iso_a.shape[3:]
    out_chan = weight_iso_b.shape[4]
    flip = xs % 8 == 0
    shape = (depth, third_rows, xs, out_chan) if flip else (third_rows, xs, depth, out_chan)
    out = pl.pallas_call(
        functools.partial(cube_kernel, (dests, zl, third_rows, vb, in_chan, mid_chan, out_chan, flip)),
        out_shape=jax.ShapeDtypeStruct(shape, BF16),
        in_specs=[VMEM] * (dests + 5),
        out_specs=VMEM,
        scratch_shapes=[
            pltpu.VMEM((4, third_rows // 2 + 1, xs + 4, depth, 3 * in_chan), BF16),
            pltpu.VMEM((third_rows + 2, xs + 2, depth, mid_chan), BF16),
            pltpu.VMEM((4, third_rows // 2, xs + 2, depth, 3 * mid_chan), BF16),
            pltpu.VMEM((2, 4, max(3 * (xs + 2), 4 * xs) * depth, mid_chan), F32),
        ],
        compiler_params=pltpu.CompilerParams(vmem_limit_bytes=(36 if depth <= 16 else 60) << 20),
        name="cubes",
    )(*near, *far, ua, bias_iso_a[None], ub, bias_iso_b[None], sums)
    return out if flip else jnp.transpose(out, (2, 0, 1, 3))


def solution(mesh):
    placed = (P("gz", "xy", None), P(), P(), P(), P(), P(), P(), P(), P(), P(), P())
    return jax.shard_map(
        body, mesh=mesh, in_specs=placed, out_specs=P(None, "xy", "gz", None), check_vma=False
    )
```
